512 devices in a mesh: vocab: 128 (over z, y, core), rows: 4 (over x).
Axes of the slice: x: 4, y: 8, z: 8, core: 2. Of those that a mesh axis runs over, the one named last changes fastest.
Arguments:
- target_hidden: bfloat16 [256, 8192], P('vocab', 'rows'), may hold values from -70 to 70
- target_head: bfloat16 [81920, 8192], P('vocab', 'rows'), may hold values from -0.1875 to 0.1875
- draft_hidden: bfloat16 [256, 8192], P('vocab', 'rows'), may hold values from -70 to 70
- draft_head: bfloat16 [32768, 8192], P('vocab', 'rows'), may hold values from -0.1875 to 0.1875
- draft_map: int32 [32768], P('vocab'), may hold values from 0 to 40959, as said below
- draft_valid: int32 [32768], P('vocab'), may hold values 0 or 1
- loss_scale: float32 [], replicated, may hold values from 2048 to 8192
Outputs:
- row_loss: float32 [256], P('rows')
- grad_hidden: bfloat16 [256, 8192], P('vocab', 'rows')
- grad_head: bfloat16 [32768, 8192], P('vocab', 'rows')
The draws below stay inside these ranges and needn't reach their ends.
Inputs may be any that keep to these rules, and one draw needn't show every extreme that they name: `draft_map`: each aligned block of 128 draft ids maps one to one onto the 128 ids of one target tile (target ids 128 t to 128 t + 127); the target tile rises strictly from block to block; every index of vocab below half of the axis owns exactly 4 used target tiles, the other indices none; the last of the owning indices always uses its highest tile.
All inputs are finite; a program needn't handle non-finite values. No bound on the sum of `draft_valid` on one device may be relied on, other than what follows from the above.
Results may differ from the reference program's by a relative error of at most 0.0225.
Values may be sent and summed in bfloat16 or wider, within the bound.
A program may use at most 64 MiB of HBM per device.

```python
import math
import jax
import jax.numpy as jnp
from jax import lax

D = 8192
VT_DEV = 640
TILE = 128
SEND_CAP = 4
ROWS = 256
VT = 81920
VT_LIVE = 81600
VD = 32768


def row_scales(key, rows, low, high):
    return jnp.exp(jax.random.uniform(key, (rows, 1), jnp.float32, math.log(low), math.log(high)))


def draw_target_hidden(key, part):
    key = jax.random.fold_in(key, 5)
    key_base, key_scale = jax.random.split(key, 2)
    base_draw = jax.random.truncated_normal(key_base, -4.0, 4.0, (ROWS, D), jnp.float32)
    row_scale = row_scales(key_scale, ROWS, 0.5, 2.0)
    return (base_draw * row_scale).astype(jnp.bfloat16)


def draw_draft_hidden(key, part):
    key = jax.random.fold_in(key, 7)
    key_base, key_scale = jax.random.split(key, 2)
    base_draw = jax.random.truncated_normal(key_base, -4.0, 4.0, (ROWS, D), jnp.float32)
    row_scale = row_scales(key_scale, ROWS, 0.5, 2.0)
    return (base_draw * row_scale).astype(jnp.bfloat16)


def draw_draft_map(key, part):
    key = jax.random.fold_in(key, 11)
    key_scores, key_columns = jax.random.split(key, 2)
    devices = VT // VT_DEV
    tiles_dev = VT_DEV // TILE
    draft_tiles = VD // TILE
    position_all = jnp.arange(devices, dtype=jnp.int32)
    counts = jnp.where(position_all < devices // 2, jnp.int32(SEND_CAP), jnp.int32(0)).astype(jnp.int32)
    local_ids = jnp.arange(tiles_dev, dtype=jnp.int32)
    scores = jax.random.randint(key_scores, (devices, tiles_dev), 0, 1 << 16, dtype=jnp.int32) * tiles_dev + local_ids[None, :]
    forced = (position_all[:, None] == devices // 2 - 1) & (local_ids[None, :] == tiles_dev - 1)
    scores = jnp.where(forced, jnp.int32(-1), scores).astype(jnp.int32)
    ranking = jnp.sum((scores[:, None, :] < scores[:, :, None]).astype(jnp.int32), axis=2).astype(jnp.int32)
    used = (ranking < counts[:, None]).reshape(-1)
    position = (jnp.cumsum(used.astype(jnp.int32)) - 1).astype(jnp.int32)
    target_slot = jnp.where(used, position, jnp.int32(draft_tiles)).astype(jnp.int32)
    tile_ids = jnp.zeros((draft_tiles,), jnp.int32).at[target_slot].set(jnp.arange(devices * tiles_dev, dtype=jnp.int32), mode='drop')
    columns = jax.vmap(lambda sub_key: jax.random.permutation(sub_key, TILE))(jax.random.split(key_columns, draft_tiles))
    return (tile_ids[:, None] * TILE + columns.astype(jnp.int32)).reshape(-1).astype(jnp.int32)


def plant(entries, own_key, smallest, top_value):
    longest = entries.shape.index(max(entries.shape))
    spots = []
    for shift in (0, 1):
        where = [jax.random.randint(jax.random.fold_in(own_key, axis), (), 0, length) for axis, length in enumerate(entries.shape)]
        where[longest] = (where[longest] + shift) % entries.shape[longest]
        spots.append(tuple(where))
    return entries.at[spots[0]].set(smallest).at[spots[1]].set(top_value)


def level_of(rng, shape, pieces, smallest, top_value):
    def one(dim, blocks):
        heights = jax.random.uniform(jax.random.fold_in(jax.random.fold_in(rng, 6), dim), (blocks,), jnp.float32, smallest / len(pieces), top_value / len(pieces))
        return jnp.repeat(jnp.exp(heights), shape[dim] // blocks).reshape((-1,) + (1,) * (len(shape) - dim - 1))

    gain = one(*pieces[0])
    for cut in pieces[1:]:
        gain = gain * one(*cut)
    return gain


def gaussian(stream_key, dims, scale, bound, pieces=(), kind=jnp.bfloat16):
    entries = jax.random.normal(stream_key, dims, jnp.float32) * scale
    if len(pieces) > 0:
        entries = level_of(stream_key, dims, pieces, -0.22, 0.18) * entries
    return jnp.clip(entries, min=-bound, max=bound).astype(kind)


def setup_inputs(seed: int = 0) -> dict:
    splits = jax.random.split(jax.random.key(seed), 8)
    target_hidden = draw_target_hidden(jax.random.fold_in(splits[7], 71), 0)
    target_head = gaussian(splits[1], (VT, D), (D // 9) ** -0.5, 0.1875, ((0, 128), (1, 4)))
    draft_hidden = draw_draft_hidden(jax.random.fold_in(splits[7], 71), 0)
    draft_head = gaussian(splits[3], (VD, D), (D // 9) ** -0.5, 0.1875, ((0, 128), (1, 4)))
    draft_map = draw_draft_map(jax.random.fold_in(splits[7], 71), 0)
    draft_valid = plant((jax.random.randint(splits[5], (VD,), 0, 32) < 31).astype(jnp.int32), jax.random.fold_in(splits[5], 1), 0, 1)
    loss_scale = jnp.clip(jnp.exp(jax.random.uniform(splits[6], (), jnp.float32, math.log(2048.0), math.log(8192.0))), 2048.0, 8192.0)
    return {"target_hidden": target_hidden, "target_head": target_head, "draft_hidden": draft_hidden, "draft_head": draft_head, "draft_map": draft_map, "draft_valid": draft_valid, "loss_scale": loss_scale}


def reference(target_hidden, target_head, draft_hidden, draft_head, draft_map, draft_valid, loss_scale):
    contract = (((1,), (1,)), ((), ()))
    live_cols = (jnp.arange(VT) < VT_LIVE)[None, :]
    target_logits = lax.dot_general(target_hidden, target_head, contract, preferred_element_type=jnp.float32)
    target_max = jnp.max(jnp.where(live_cols, target_logits, -jnp.inf), axis=1, keepdims=True)
    target_exp = jnp.where(live_cols, jnp.exp(target_logits - target_max), jnp.float32(0.0))
    target_total = jnp.sum(target_exp, axis=1, keepdims=True)
    target_prob = (target_exp / target_total).astype(jnp.bfloat16)
    valid_cols = (draft_valid > 0)[None, :]
    mapped = jnp.take(target_prob, draft_map.astype(jnp.int32), axis=1)
    soft_target = jnp.where(valid_cols, mapped, jnp.zeros_like(mapped)).astype(jnp.bfloat16)
    draft_logits = lax.dot_general(draft_hidden, draft_head, contract, preferred_element_type=jnp.float32)
    draft_max = jnp.max(jnp.where(valid_cols, draft_logits, -jnp.inf), axis=1, keepdims=True)
    draft_exp = jnp.where(valid_cols, jnp.exp(draft_logits - draft_max), jnp.float32(0.0))
    draft_total = jnp.sum(draft_exp, axis=1, keepdims=True)
    draft_lse = draft_max + jnp.log(draft_total)
    soft_wide = soft_target.astype(jnp.float32)
    target_mass = jnp.sum(soft_wide, axis=1, keepdims=True)
    cross_term = jnp.sum(soft_wide * draft_logits, axis=1, keepdims=True)
    row_loss = (target_mass * draft_lse - cross_term)[:, 0]
    grad_value = loss_scale * (jnp.exp(draft_logits - draft_lse) * target_mass - soft_wide)
    logit_grad = jnp.where(valid_cols, grad_value, jnp.float32(0.0)).astype(jnp.bfloat16)
    grad_hidden = jnp.dot(logit_grad, draft_head, preferred_element_type=jnp.float32).astype(jnp.bfloat16)
    grad_head = lax.dot_general(logit_grad, draft_hidden, (((0,), (0,)), ((), ())), preferred_element_type=jnp.float32).astype(jnp.bfloat16)
    return row_loss, grad_hidden, grad_head
```

```python
import functools
import math

import jax
import jax.numpy as jnp
from jax import lax
from jax.experimental import pallas as pl
from jax.experimental.pallas import tpu as pltpu
from jax.sharding import PartitionSpec as P

MESH = pl.DeviceIdType.MESH
FAR_BELOW = -1e30
L = 128
NT = (((1,), (1,)), ((), ()))
TN = (((0,), (0,)), ((), ()))
NN = (((1,), (0,)), ((), ()))
BF = jnp.bfloat16
F32 = jnp.float32


def matmul(a, b, dims):
    return lax.dot_general(a, b, dims, preferred_element_type=F32)


def iota(shape, dim):
    return lax.broadcasted_iota(jnp.int32, shape, dim)


class Sizes:
    def __init__(self, vocab, rows, th, thead, dhead):
        self.V, self.X = vocab, rows
        self.Z = self.Y = math.isqrt(vocab // 2)
        self.R0, self.F = th
        self.G = self.R0 * self.Z
        self.nk = self.G // self.R0
        self.W = self.F // self.nk
        self.H = self.F // 2
        self.W2 = self.H // self.nk
        self.VT, self.VD = thead[0], dhead[0]
        self.ROWS = self.R0 * vocab
        self.CH = self.ROWS // rows
        self.SPC = self.CH // self.G


def body(
    s,
    th, dh, thead_hbm, dhead_hbm, dmap, dvalid, scale,
    loss_out, gh_out, ghead_out,
    thead, dhead, stage, stage_big, t0, d0, a_t, a_d, map_own, map_in, sel,
    tp, tr, dfull, dp, dr, ld, s_out, s_in, st_own, st_in, f0, f1, f2, c0, c1, c2,
    ga_t, ga_d, keep_t, keep_d, js_t, js_d, jr_t, jr_d, q_t, q_d, qr_t, qr_d,
    w_out, w_in, ghead,
    sem_head, sem_l1s, sem_l1r, sem_rs, sem_rr, sem_sibs, sem_sibr, sem_ms, sem_mr,
    sem_ts, sem_tr, sem_ds, sem_dr, sem_ss, sem_sr, sem_fs, sem_fr, sem_cs, sem_cr,
    sem_gs, sem_gr, sem_js, sem_jr, sem_qs, sem_qr, sem_ws, sem_wr, sem_out,
):
    V, X, Z, Y, R0, G, nk, W, H, W2 = s.V, s.X, s.Z, s.Y, s.R0, s.G, s.nk, s.W, s.H, s.W2
    v = lax.axis_index("vocab")
    x = lax.axis_index("rows")
    c = lax.rem(v, 2)
    chip = lax.div(v, 2)
    y = lax.rem(chip, Y)
    z = lax.div(chip, Y)
    sib = v + 1 - 2 * c

    def at(zz, yy, cc):
        return (zz * Y + yy) * 2 + cc

    def y_peer(k):
        return at(z, lax.rem(y + k, Y), c)

    def z_peer(k):
        return at(lax.rem(z + k, Z), y, c)

    def x_peer(k):
        return lax.rem(x + k, X)

    def rcopy(src, dst, ssem, rsem, vv, xx):
        return pltpu.make_async_remote_copy(
            src_ref=src, dst_ref=dst, send_sem=ssem, recv_sem=rsem,
            device_id=(vv, xx), device_id_type=MESH,
        )

    sends = []

    def send(src, dst, ssem, rsem, vv, xx=None):
        cp = rcopy(src, dst, ssem, rsem, vv, x if xx is None else xx)
        cp.start()
        sends.append(cp)

    def arrived(dst, rsem):
        rcopy(dst, dst, rsem, rsem, sib, x).wait_recv()

    load_t = pltpu.make_async_copy(thead_hbm, thead, sem_head.at[0])
    load_d = pltpu.make_async_copy(dhead_hbm, dhead, sem_head.at[1])
    load_t.start()
    load_d.start()

    owner = v < V // 2
    owner_of = lax.div(v, 2)

    barrier = pltpu.get_barrier_semaphore()

    def hello(vv, xx):
        pl.semaphore_signal(barrier, inc=1, device_id=(vv, xx), device_id_type=MESH)

    for k in range(1, Y):
        hello(y_peer(k), x)
    for k in range(1, Z):
        hello(z_peer(k), x)
    hello(sib, x)
    for k in range(1, X):
        hello(v, x_peer(k))

    @pl.when(v > 0)
    def _():
        hello(owner_of, x)

    @pl.when(owner)
    def _():
        hello(2 * v + 1, x)

    @pl.when(jnp.logical_and(owner, v > 0))
    def _():
        hello(2 * v, x)

    for ref, dst, slot in ((th, t0, y), (dh, d0, z)):
        for k in range(nk):
            for a in range(W // L):
                cols = slice(k * W + a * L, k * W + (a + 1) * L)
                stage[a, pl.ds(k, R0, stride=nk), :] = ref[:, cols].astype(F32)
        for a in range(W // L):
            dst[slot, :, a * L:(a + 1) * L] = stage[a].astype(BF)
    masked_map = jnp.where(dvalid[...] > 0, dmap[...], -1)
    map_own[...] = jnp.broadcast_to(masked_map, map_own.shape)

    live_owner = owner.astype(jnp.int32)
    live_v = (v > 0).astype(jnp.int32)
    pl.semaphore_wait(
        barrier, (Y - 1) + (Z - 1) + 1 + (X - 1) + live_v + live_owner * (1 + live_v)
    )

    for k in range(1, Y):
        send(t0.at[y], t0.at[y], sem_l1s.at[0, k], sem_l1r.at[0, k], y_peer(k))
        send(d0.at[z], d0.at[z], sem_l1s.at[1, k], sem_l1r.at[1, k], z_peer(k))

    @pl.when(v > 0)
    def _():
        rcopy(map_own, map_in.at[c], sem_ms, sem_mr.at[c], owner_of, x).start()

    @pl.when(v == 0)
    def _():
        map_in[0] = map_own[...]

    def relayout(src, dst, slot):
        for i in range(Y):
            for a in range(W // L):
                stage_big[a, i * G:(i + 1) * G, :] = src[i, :, a * L:(a + 1) * L].astype(F32)
        for k in range(nk):
            for a in range(W // L):
                cols = slice(k * W + a * L, k * W + (a + 1) * L)
                dst[slot, :, cols] = stage_big[a, pl.ds(k, G, stride=nk), :].astype(BF)

    for k in range(1, Y):
        arrived(t0.at[lax.rem(y + Y - k, Y)], sem_l1r.at[0, k])
    relayout(t0, a_t, z * 2 + c)

    half = Z // 2

    def ring_slot(q, n):
        return lax.rem(q + 2 * n, n) * 2 + c

    rings = (
        (0, a_t, z, Z, z_peer),
        (1, a_d, y, Y, y_peer),
    )

    def part(buf, slot, direction, step):
        if step < half:
            return buf.at[slot]
        return buf.at[slot, :, pl.ds(0, H)] if direction == 0 else buf.at[slot, :, pl.ds(H, H)]

    def ring_send(ring, step):
        i, buf, pos, n, peer = rings[ring]
        for direction in (0, 1):
            q = pos - step + 1 if direction == 0 else pos + step - 1
            ref = part(buf, ring_slot(q, n), direction, step)
            send(
                ref, ref, sem_rs.at[i, direction, step - 1], sem_rr.at[i, direction, step - 1],
                peer(1 if direction == 0 else n - 1),
            )

    def ring_wait(ring, step):
        i, buf, pos, n, _ = rings[ring]
        for direction in (0, 1):
            q = pos - step if direction == 0 else pos + step
            arrived(
                part(buf, ring_slot(q, n), direction, step), sem_rr.at[i, direction, step - 1]
            )

    def sib_refs(ring, step, core):
        i, buf, pos, n, _ = rings[ring]
        if step == 0:
            return [(buf.at[lax.rem(pos, n) * 2 + core], 0)]
        if step == half:
            return [(buf.at[lax.rem(pos + half, n) * 2 + core], 2 * half - 1)]
        return [
            (buf.at[lax.rem(pos - step + n, n) * 2 + core], 2 * step - 1),
            (buf.at[lax.rem(pos + step, n) * 2 + core], 2 * step),
        ]

    def sib_send(ring, step):
        for ref, k in sib_refs(ring, step, c):
            send(ref, ref, sem_sibs.at[ring, k], sem_sibr.at[ring, k], sib)

    def sib_wait(ring, step):
        for ref, k in sib_refs(ring, step, 1 - c):
            arrived(ref, sem_sibr.at[ring, k])

    ring_send(0, 1)
    sib_send(0, 0)
    for k in range(1, Z):
        arrived(d0.at[lax.rem(z + Z - k, Z)], sem_l1r.at[1, k])
    relayout(d0, a_d, y * 2 + c)
    ring_send(1, 1)
    sib_send(1, 0)

    @pl.when(v > 0)
    def _():
        rcopy(map_own, map_in.at[c], sem_ms, sem_mr.at[c], owner_of, x).wait_send()

    @pl.when(owner)
    def _():
        arrived(map_in.at[1], sem_mr.at[1])

        @pl.when(v > 0)
        def _():
            arrived(map_in.at[0], sem_mr.at[0])

        ids = iota((s.VT, s.VD), 0) + v * s.VT
        for i in range(2):
            hit = ids == jnp.broadcast_to(map_in[i, 0:1, :], (s.VT, s.VD))
            sel[:, i * s.VD:(i + 1) * s.VD] = jnp.where(hit, 1.0, 0.0).astype(BF)

    load_t.wait()

    def target_chunk(r):
        block = a_t[pl.ds(r * s.SPC, s.SPC)].reshape(s.CH, s.F)
        tp[r] = matmul(block, thead[...], NT)
        k = lax.rem(x - r + X, X)

        @pl.when(r != x)
        def _():
            rcopy(tp.at[r], tr.at[k], sem_ts.at[k], sem_tr.at[k], v, r).start()

    own = lax.div(z * 2, s.SPC)
    if X == 4 and Z == 8:
        sign = 1 - 2 * lax.rem(z, 2)
        order = [(1, own), (2, lax.rem(own - sign + X, X)), (3, lax.rem(own + sign + X, X)),
                 (4, lax.rem(own + 2, X))]
    else:
        order = [(half, lax.rem(own + k, X)) for k in range(X)]
    for step in range(0, half + 1):
        if step > 0:
            for ring in (0, 1):
                ring_wait(ring, step)
                if step < half:
                    ring_send(ring, step + 1)
                sib_send(ring, step)
        sib_wait(0, step)
        for when_, r in order:
            if when_ == step:
                target_chunk(r)
        sib_wait(1, step)

    load_d.wait()
    d_part = matmul(a_d[...].reshape(s.ROWS, s.F), dhead[...], NT)
    for a in range(s.VD // L):
        dfull[a] = d_part[:, a * L:(a + 1) * L]
    zpx = Z // X
    for zz in range(Z):
        for cc in range(2):
            for j in range(R0):
                to = pl.ds(((zz % zpx) * 2 + cc) * G + j, Y, stride=R0)
                for a in range(s.VD // L):
                    dp[zz // zpx, a, to, :] = dfull[
                        a, pl.ds((cc * Z + zz) * R0 + j, Y, stride=2 * G), :
                    ]
    for k in range(1, X):
        send(dp.at[lax.rem(x - k + X, X)], dr.at[k], sem_ds.at[k], sem_dr.at[k], v,
             lax.rem(x - k + X, X))

    for k in range(1, X):
        arrived(tr.at[k], sem_tr.at[k])
    lt = tp[x]
    for k in range(1, X):
        lt = lt + tr[k]
    live_limit = s.VT * V - s.VT // 2
    live = iota((1, s.VT), 1) + v * s.VT < live_limit
    tm = jnp.max(jnp.where(live, lt, FAR_BELOW), axis=1, keepdims=True)
    te = jnp.where(live, jnp.exp(lt - tm), 0.0)
    ts = jnp.sum(te, axis=1, keepdims=True)

    s_out[...] = jnp.zeros_like(s_out)

    @pl.when(owner)
    def _():
        te16 = te.astype(BF)
        for i in range(2):
            s_out[i] = matmul(te16, sel[:, i * s.VD:(i + 1) * s.VD], NN).astype(BF)

    mass_here = jnp.sum(s_out[0].astype(F32) + s_out[1].astype(F32), axis=1, keepdims=True)

    eye = iota((s.CH, 128), 0) == iota((s.CH, 128), 1)

    def to_row(col):
        return jnp.sum(jnp.where(eye, col, 0.0), axis=0, keepdims=True)

    def to_col(row):
        return jnp.sum(jnp.where(eye, row, 0.0), axis=1, keepdims=True)

    st_own[...] = jnp.broadcast_to(to_row(tm), st_own.shape)

    @pl.when(owner)
    def _():
        rcopy(s_out.at[1], s_in, sem_ss.at[1], sem_sr.at[0], 2 * v + 1, x).start()
        rcopy(st_own, st_in, sem_ss.at[3], sem_sr.at[1], 2 * v + 1, x).start()

        @pl.when(v > 0)
        def _():
            rcopy(s_out.at[0], s_in, sem_ss.at[0], sem_sr.at[0], 2 * v, x).start()
            rcopy(st_own, st_in, sem_ss.at[2], sem_sr.at[1], 2 * v, x).start()

        @pl.when(v == 0)
        def _():
            s_in[...] = s_out[0]
            st_in[...] = st_own[...]

    valid = dvalid[...] > 0
    for k in range(1, X):
        arrived(dr.at[k], sem_dr.at[k])
    l_d = dp[x]
    for k in range(1, X):
        l_d = l_d + dr[k]
    l_d = jnp.concatenate([l_d[a] for a in range(s.VD // L)], axis=1)
    ld[...] = l_d
    dm = jnp.max(jnp.where(valid, l_d, FAR_BELOW), axis=1, keepdims=True)
    ds = jnp.sum(jnp.where(valid, jnp.exp(l_d - dm), 0.0), axis=1, keepdims=True)

    zero_row = jnp.zeros((5, 128), F32)
    tmr = to_row(tm)
    maxes = jnp.concatenate([tmr, tmr, to_row(dm), zero_row], axis=0)
    sums = jnp.concatenate([to_row(ts), to_row(mass_here), to_row(ds), zero_row], axis=0)

    def exchange(buf, slot, n, peer, ssem, rsem):
        for k in range(1, n):
            send(buf.at[slot], buf.at[slot], ssem.at[k], rsem.at[k], peer(k))

    def exchange_wait(buf, slot, n, rsem):
        for k in range(1, n):
            arrived(buf.at[lax.rem(slot + n - k, n)], rsem.at[k])

    hops = (
        (f0, c0, c, 2, lambda k: sib),
        (f1, c1, y, Y, y_peer),
        (f2, c2, z, Z, z_peer),
    )
    for h, (buf, _, slot, n, peer) in enumerate(hops):
        buf[slot, 0] = maxes
        buf[slot, 1] = sums
        exchange(buf, slot, n, peer, sem_fs.at[h], sem_fr.at[h])
        exchange_wait(buf, slot, n, sem_fr.at[h])
        maxes = buf[0, 0]
        for i in range(1, n):
            maxes = jnp.maximum(maxes, buf[i, 0])
        sums = buf[0, 1] * jnp.exp(buf[0, 0] - maxes)
        for i in range(1, n):
            sums = sums + buf[i, 1] * jnp.exp(buf[i, 0] - maxes)

    @pl.when(v > 0)
    def _():
        arrived(s_in, sem_sr.at[0])
        arrived(st_in, sem_sr.at[1])

    t_max, t_total = maxes[0:1], sums[0:1]
    factor = to_col(jnp.exp(st_in[0:1] - t_max) / t_total)
    mass = to_col(sums[1:2] / t_total)
    lse = to_col(maxes[2:3] + jnp.log(sums[2:3]))
    soft = s_in[...].astype(F32) * factor
    l_d = ld[...]
    grad = scale[0, 0] * (jnp.exp(l_d - lse) * mass - soft)
    ga_t[pl.ds(x * s.SPC, s.SPC)] = (
        jnp.where(valid, grad, 0.0).astype(BF).reshape(s.SPC, G, s.VD)
    )
    for k in range(1, X):
        chunk = ga_t.at[pl.ds(x * s.SPC, s.SPC)]
        send(chunk, chunk, sem_gs.at[k], sem_gr.at[k], v, x_peer(k))

    cross = jnp.broadcast_to(to_row(jnp.sum(soft * l_d, axis=1, keepdims=True)), (8, 128))

    def cross_send(h, value):
        _, buf, slot, n, peer = hops[h]
        buf[slot] = value
        exchange(buf, slot, n, peer, sem_cs.at[h], sem_cr.at[h])

    def cross_wait(h):
        _, buf, slot, n, _ = hops[h]
        exchange_wait(buf, slot, n, sem_cr.at[h])
        total = buf[0]
        for i in range(1, n):
            total = total + buf[i]
        return total

    cross_send(0, cross)
    shape = (s.ROWS, s.ROWS)
    dpos, tpos = iota(shape, 0), iota(shape, 1)
    lr, lz = R0.bit_length() - 1, Z.bit_length() - 1
    dj = dpos & (R0 - 1)
    dz = (dpos >> lr) & (Z - 1)
    dc = (dpos >> (lr + lz)) & 1
    dy = dpos >> (lr + lz + 1)
    perm = jnp.where((((dz * 2 + dc) * Y + dy) << lr) + dj == tpos, 1.0, 0.0).astype(BF)

    cross_send(1, cross_wait(0))

    for k in range(1, X):
        other = ga_t.at[pl.ds(lax.rem(x + X - k, X) * s.SPC, s.SPC)]
        arrived(other, sem_gr.at[k])
    ga_d[...] = (
        matmul(perm, ga_t[...].reshape(s.ROWS, s.VD), NN).astype(BF).reshape(2 * Y, G, s.VD)
    )

    def rows_of(buf, core):
        return jnp.concatenate([buf[i * 2 + core] for i in range(Z)], axis=0)

    js_t[...] = matmul(rows_of(ga_t, 1 - c), dhead[:, :H], NN).astype(BF).reshape(Z, G, H)
    send(js_t, jr_t, sem_js.at[0], sem_jr.at[0], sib)
    js_d[...] = matmul(rows_of(ga_d, 1 - c), dhead[:, H:], NN).astype(BF).reshape(Y, G, H)
    send(js_d, jr_d, sem_js.at[1], sem_jr.at[1], sib)
    keep_t[...] = matmul(rows_of(ga_t, c), dhead[:, :H], NN).reshape(Z, G, H)
    keep_d[...] = matmul(rows_of(ga_d, c), dhead[:, H:], NN).reshape(Y, G, H)

    parts = (
        (0, jr_t, keep_t, q_t, qr_t, z, Z, z_peer, y, Y, y_peer),
        (1, jr_d, keep_d, q_d, qr_d, y, Y, y_peer, z, Z, z_peer),
    )
    for i, jr, keep, q, qr, pos, n, peer, _, _, _ in parts:
        arrived(jr, sem_jr.at[i])
        for k in range(1, n):
            to = lax.rem(pos + k, n)
            q[k] = (keep[to] + jr[to].astype(F32)).astype(BF)
            send(q.at[k], qr.at[k], sem_qs.at[i, k], sem_qr.at[i, k], peer(k))

    ghead[...] = matmul(ga_d[...].reshape(s.ROWS, s.VD), a_d[...].reshape(s.ROWS, s.F), TN).astype(
        BF
    )
    store = pltpu.make_async_copy(ghead, ghead_out, sem_out)
    store.start()

    cross_send(2, cross_wait(1))

    for i, jr, keep, q, qr, pos, n, peer, pos2, n2, peer2 in parts:
        total = keep[pos] + jr[pos].astype(F32)
        for k in range(1, n):
            arrived(qr.at[k], sem_qr.at[i, k])
            total = total + qr[k].astype(F32)
        for k in range(nk):
            stage_big[0, pl.ds(k, G, stride=nk), :] = total[:, k * W2:(k + 1) * W2]
        for p in range(n2):
            w_out[i, p] = stage_big[0, p * G:(p + 1) * G, :].astype(BF)
        for k in range(1, n2):
            send(
                w_out.at[i, lax.rem(pos2 + k, n2)], w_in.at[i, k],
                sem_ws.at[i, k], sem_wr.at[i, k], peer2(k),
            )
        w_in[i, 0] = w_out[i, pos2]

    total_cross = to_col(cross_wait(2)[0:1])
    loss = mass * lse - total_cross
    shape = (s.CH, 128)
    src, dst = iota(shape, 0), iota(shape, 1)
    sj = src & (R0 - 1)
    sy = (src >> lr) & (Y - 1)
    sc = (src >> (lr + lz)) & 1
    sz = src >> (lr + lz + 1)
    place = (((sz * Y + sy) * 2 + sc) << lr) + sj == dst
    loss_out[...] = jnp.sum(jnp.where(place, loss, 0.0), axis=0, keepdims=True)

    for i, jr, keep, q, qr, pos, n, peer, pos2, n2, peer2 in parts:
        total = w_in[i, 0].astype(F32)
        for k in range(1, n2):
            arrived(w_in.at[i, k], sem_wr.at[i, k])
            total = total + w_in[i, k].astype(F32)
        stage[0] = total
        for k in range(nk):
            gh_out[:, i * H + k * W2:i * H + (k + 1) * W2] = stage[
                0, pl.ds(k, R0, stride=nk), :
            ].astype(BF)

    for cp in sends:
        cp.wait_send()
    for k in range(1, X):
        rcopy(tr.at[k], tr.at[k], sem_ts.at[k], sem_ts.at[k], v, x).wait_send()

    @pl.when(owner)
    def _():
        rcopy(s_out.at[1], s_in, sem_ss.at[1], sem_sr.at[0], 2 * v + 1, x).wait_send()
        rcopy(st_own, st_in, sem_ss.at[3], sem_sr.at[1], 2 * v + 1, x).wait_send()

        @pl.when(v > 0)
        def _():
            rcopy(s_out.at[0], s_in, sem_ss.at[0], sem_sr.at[0], 2 * v, x).wait_send()
            rcopy(st_own, st_in, sem_ss.at[2], sem_sr.at[1], 2 * v, x).wait_send()

    store.wait()


def on_device(vocab, rows, th, thead, dh, dhead, dmap, dvalid, scale):
    s = Sizes(vocab, rows, th.shape, thead.shape, dhead.shape)
    Z, Y, X, G, F, H, W, W2, VT, VD, CH = (
        s.Z, s.Y, s.X, s.G, s.F, s.H, s.W, s.W2, s.VT, s.VD, s.CH
    )
    vm = pltpu.VMEM
    dma = pltpu.SemaphoreType.DMA
    scratch = [
        vm((VT, F), BF), vm((VD, F), BF),
        vm((W // L, G, L), F32), vm((W // L, G * Y, L), F32),
        vm((Y, G, W), BF), vm((Z, G, W), BF),
        vm((2 * Z, G, F), BF), vm((2 * Y, G, F), BF),
        vm((8, VD), jnp.int32), vm((2, 8, VD), jnp.int32),
        vm((VT, 2 * VD), BF),
        vm((X, CH, VT), F32), vm((X, CH, VT), F32),
        vm((VD // L, s.ROWS, L), F32),
        vm((X, VD // L, CH, L), F32), vm((X, VD // L, CH, L), F32),
        vm((CH, VD), F32),
        vm((2, CH, VD), BF), vm((CH, VD), BF),
        vm((8, 128), F32), vm((8, 128), F32),
        vm((2, 2, 8, 128), F32), vm((Y, 2, 8, 128), F32), vm((Z, 2, 8, 128), F32),
        vm((2, 8, 128), F32), vm((Y, 8, 128), F32), vm((Z, 8, 128), F32),
        vm((2 * Z, G, VD), BF), vm((2 * Y, G, VD), BF),
        vm((Z, G, H), F32), vm((Y, G, H), F32),
        vm((Z, G, H), BF), vm((Y, G, H), BF),
        vm((Z, G, H), BF), vm((Y, G, H), BF),
        vm((Z, G, H), BF), vm((Y, G, H), BF),
        vm((Z, G, H), BF), vm((Y, G, H), BF),
        vm((2, Y, G, W2), BF), vm((2, Y, G, W2), BF),
        vm((VD, F), BF),
        dma((2,)),
        dma((2, Y)), dma((2, Y)),
        dma((2, 2, Z // 2)), dma((2, 2, Z // 2)),
        dma((2, Z)), dma((2, Z)),
        dma, dma((2,)),
        dma((X,)), dma((X,)), dma((X,)), dma((X,)),
        dma((4,)), dma((2,)),
        dma((3, Z)), dma((3, Z)), dma((3, Z)), dma((3, Z)),
        dma((X,)), dma((X,)),
        dma((2,)), dma((2,)), dma((2, Z)), dma((2, Z)), dma((2, Z)), dma((2, Z)),
        dma,
    ]
    any_ = pl.BlockSpec(memory_space=pl.ANY)
    vmem = pl.BlockSpec(memory_space=pltpu.VMEM)
    smem = pl.BlockSpec(memory_space=pltpu.SMEM)
    loss, gh, ghead = pl.pallas_call(
        functools.partial(body, s),
        out_shape=(
            jax.ShapeDtypeStruct((1, 128), F32),
            jax.ShapeDtypeStruct((s.R0, F), BF),
            jax.ShapeDtypeStruct((VD, F), BF),
        ),
        in_specs=[vmem, vmem, any_, any_, vmem, vmem, smem],
        out_specs=(vmem, vmem, any_),
        scratch_shapes=scratch,
        compiler_params=pltpu.CompilerParams(
            collective_id=0, has_side_effects=True, vmem_limit_bytes=48 * 1024 * 1024
        ),
    )(th, dh, thead, dhead, dmap.reshape(1, VD), dvalid.reshape(1, VD), scale.reshape(1, 1))
    return loss[0, :CH], gh, ghead


def solution(mesh):
    both, one = P("vocab", "rows"), P("vocab")
    return jax.shard_map(
        functools.partial(on_device, mesh.shape["vocab"], mesh.shape["rows"]),
        mesh=mesh,
        in_specs=(both, both, both, both, one, one, P()),
        out_specs=(P("rows"), both, both),
        check_vma=False,
    )
```

```python
import functools
import math

import jax
import jax.numpy as jnp
from jax import lax
from jax.experimental import pallas as pl
from jax.experimental.pallas import tpu as pltpu
from jax.sharding import PartitionSpec as P

MESH = pl.DeviceIdType.MESH
FAR_BELOW = -1e30
L = 128
NT = (((1,), (1,)), ((), ()))
TN = (((0,), (0,)), ((), ()))
NN = (((1,), (0,)), ((), ()))
BF = jnp.bfloat16
F32 = jnp.float32


def matmul(a, b, dims):
    return lax.dot_general(a, b, dims, preferred_element_type=F32)


def iota(shape, dim):
    return lax.broadcasted_iota(jnp.int32, shape, dim)


class Sizes:
    def __init__(self, vocab, rows, th, thead, dhead):
        self.V, self.X = vocab, rows
        self.Z = self.Y = math.isqrt(vocab // 2)
        self.R0, self.F = th
        self.G = self.R0 * self.Z
        self.nk = self.G // self.R0
        self.W = self.F // self.nk
        self.H = self.F // 2
        self.W2 = self.H // self.nk
        self.VT, self.VD = thead[0], dhead[0]
        self.ROWS = self.R0 * vocab
        self.CH = self.ROWS // rows
        self.SPC = self.CH // self.G


def body(
    s,
    th_hbm, dh_hbm, thead_hbm, dhead_hbm, dmap_hbm, dvalid_hbm, scale,
    loss_out, gh_out, ghead_out,
    th, dh, dmap, dvalid, thead, dhead, stage, stage_big, t0, d0, a_t, a_d, map_own, map_in, sel,
    tp0, tp1, tp2, tr0, tr1, tr2, tfull, dp, dr, ld, s_out, s_in, st_own, st_in, f0, f1, f2, c0, c1, c2,
    ga_t, ga_d, keep_t, keep_d, js_t, js_d, jr_t, jr_d, q_t, q_d, qr_t, qr_d,
    w_out, w_in, ghead,
    sem_head, sem_l1s, sem_l1r, sem_rs, sem_rr, sem_sibs, sem_sibr, sem_ms, sem_mr,
    sem_ts, sem_tr, sem_ds, sem_dr, sem_ss, sem_sr, sem_fs, sem_fr, sem_cs, sem_cr,
    sem_gs, sem_gr, sem_js, sem_jr, sem_qs, sem_qr, sem_ws, sem_wr, sem_out,
):
    V, X, Z, Y, R0, G, nk, W, H, W2 = s.V, s.X, s.Z, s.Y, s.R0, s.G, s.nk, s.W, s.H, s.W2
    v = lax.axis_index("vocab")
    x = lax.axis_index("rows")
    c = lax.rem(v, 2)
    chip = lax.div(v, 2)
    y = lax.rem(chip, Y)
    z = lax.div(chip, Y)
    sib = v + 1 - 2 * c

    def at(zz, yy, cc):
        return (zz * Y + yy) * 2 + cc

    def y_peer(k):
        return at(z, lax.rem(y + k, Y), c)

    def z_peer(k):
        return at(lax.rem(z + k, Z), y, c)

    def x_peer(k):
        return lax.rem(x + k, X)

    def rcopy(src, dst, ssem, rsem, vv, xx):
        return pltpu.make_async_remote_copy(
            src_ref=src, dst_ref=dst, send_sem=ssem, recv_sem=rsem,
            device_id=(vv, xx), device_id_type=MESH,
        )

    tp, tr = (tp0, tp1, tp2), (tr0, tr1, tr2)
    sends = []
    drains = []

    def send(src, dst, ssem, rsem, vv, xx=None):
        cp = rcopy(src, dst, ssem, rsem, vv, x if xx is None else xx)
        cp.start()
        sends.append(cp)

    def arrived(dst, rsem):
        rcopy(dst, dst, rsem, rsem, sib, x).wait_recv()

    def finish():
        for cp in sends:
            cp.wait_send()
        for drain in drains:
            drain()

    small = [
        pltpu.make_async_copy(src, dst, sem_head.at[2 + i])
        for i, (src, dst) in enumerate(
            ((th_hbm, th), (dh_hbm, dh), (dmap_hbm, dmap), (dvalid_hbm, dvalid))
        )
    ]
    for cp in small:
        cp.start()
    load_t = pltpu.make_async_copy(thead_hbm, thead, sem_head.at[0])
    load_d = pltpu.make_async_copy(dhead_hbm, dhead, sem_head.at[1])
    load_t.start()
    load_d.start()

    owner = v < V // 2
    owner_of = lax.div(v, 2)

    barrier = pltpu.get_barrier_semaphore()

    def hello(vv, xx):
        pl.semaphore_signal(barrier, inc=1, device_id=(vv, xx), device_id_type=MESH)

    for k in range(1, Y):
        hello(y_peer(k), x)
    for k in range(1, Z):
        hello(z_peer(k), x)
    hello(sib, x)
    for k in range(1, X):
        hello(v, x_peer(k))

    @pl.when(v > 0)
    def _():
        hello(owner_of, x)

    @pl.when(owner)
    def _():
        hello(2 * v + 1, x)

    @pl.when(jnp.logical_and(owner, v > 0))
    def _():
        hello(2 * v, x)

    for cp in small:
        cp.wait()

    for ref, dst, slot in ((th, t0, z), (dh, d0, y)):
        for k in range(nk):
            for a in range(W // L):
                cols = slice(k * W + a * L, k * W + (a + 1) * L)
                stage[a, pl.ds(k, R0, stride=nk), :] = ref[:, cols].astype(F32)
        for a in range(W // L):
            dst[slot, :, a * L:(a + 1) * L] = stage[a].astype(BF)
    masked_map = jnp.where(dvalid[...] > 0, dmap[...], -1)
    map_own[...] = jnp.broadcast_to(masked_map, map_own.shape)

    live_owner = owner.astype(jnp.int32)
    live_v = (v > 0).astype(jnp.int32)
    pl.semaphore_wait(
        barrier, (Y - 1) + (Z - 1) + 1 + (X - 1) + live_v + live_owner * (1 + live_v)
    )

    for k in range(1, Z):
        send(t0.at[z], t0.at[z], sem_l1s.at[0, k], sem_l1r.at[0, k], z_peer(k))
        send(d0.at[y], d0.at[y], sem_l1s.at[1, k], sem_l1r.at[1, k], y_peer(k))

    @pl.when(v > 0)
    def _():
        rcopy(map_own, map_in.at[c], sem_ms, sem_mr.at[c], owner_of, x).start()

    def drain_map():
        @pl.when(v > 0)
        def _():
            rcopy(map_own, map_in.at[c], sem_ms, sem_mr.at[c], owner_of, x).wait_send()

    drains.append(drain_map)

    @pl.when(v == 0)
    def _():
        map_in[0] = map_own[...]

    def relayout(src, dst, slot):
        for i in range(Y):
            for a in range(W // L):
                stage_big[a, i * G:(i + 1) * G, :] = src[i, :, a * L:(a + 1) * L].astype(F32)
        for k in range(nk):
            for a in range(W // L):
                cols = slice(k * W + a * L, k * W + (a + 1) * L)
                dst[slot, :, cols] = stage_big[a, pl.ds(k, G, stride=nk), :].astype(BF)

    for k in range(1, Z):
        arrived(t0.at[lax.rem(z + Z - k, Z)], sem_l1r.at[0, k])
    relayout(t0, a_t, 0)

    hop = (2, -2, 1, -1, 1, -1, 2, -2)
    held = (0, 0, 0, 0, -2, 2, -2, 2)
    if Z == 8:
        first_kinds, next_kinds = (0, 1, 2, 3), {0: (4, 6), 1: (5, 7)}
        turns, stages = (0, -2, 2, -1, 1, -3, 3, 4), (0, 5, 7, 8)
    else:
        first_kinds, next_kinds = (2,), {}
        turns, stages = (0, 1), (0, 2)

    def turn_slot(ring, turn, core):
        if ring == 1:
            return lax.rem(z + turn + Z, Z) * 2 + core
        near = [i for i, other in enumerate(turns) if (other - turn) % Y == 0]
        return near[0] * 2 + (0 if core is c else 1)

    def block_of(ring, turn, kind, core):
        buf, slot = (a_t, a_d)[ring], turn_slot(ring, turn, core)
        if kind is None or kind < 6:
            return buf.at[slot]
        return buf.at[slot, :, pl.ds(0, H)] if kind == 6 else buf.at[slot, :, pl.ds(H, H)]

    def ring_send(ring, kind):
        src = block_of(ring, held[kind], kind, c)
        dst = src if ring == 1 else block_of(ring, held[kind] - hop[kind], kind, c)
        send(src, dst, sem_rs.at[ring, kind], sem_rr.at[ring, kind],
             (y_peer, z_peer)[ring](hop[kind] % Z))

    def ring_wait(ring, kind):
        arrived(block_of(ring, held[kind] - hop[kind], kind, c), sem_rr.at[ring, kind])

    def sib_turn(kind):
        return 0 if kind is None else held[kind] - hop[kind]

    def sib_send(ring, kind):
        turn, k = sib_turn(kind), 7 if kind is None else kind
        src = block_of(ring, turn, None, c)
        dst = src if ring == 1 else block_of(ring, turn, None, 1 - c)
        send(src, dst, sem_sibs.at[ring, k], sem_sibr.at[ring, k], sib)

    def sib_wait(ring, kind):
        k = 7 if kind is None else kind
        arrived(block_of(ring, sib_turn(kind), None, 1 - c), sem_sibr.at[ring, k])

    def ring_start(ring):
        for kind in first_kinds:
            ring_send(ring, kind)
        sib_send(ring, None)

    ring_start(0)
    for k in range(1, Y):
        arrived(d0.at[lax.rem(y + Y - k, Y)], sem_l1r.at[1, k])
    relayout(d0, a_d, z * 2 + c)
    ring_start(1)

    @pl.when(owner)
    def _():
        arrived(map_in.at[1], sem_mr.at[1])

        @pl.when(v > 0)
        def _():
            arrived(map_in.at[0], sem_mr.at[0])

        ids = iota((s.VT, s.VD), 0) + v * s.VT
        for i in range(2):
            hit = ids == jnp.broadcast_to(map_in[i, 0:1, :], (s.VT, s.VD))
            sel[:, i * s.VD:(i + 1) * s.VD] = jnp.where(hit, 1.0, 0.0).astype(BF)

    load_t.wait()

    zpx = Z // X
    per = zpx * R0

    def target_stage(st):
        lo, hi = stages[st] * 2, stages[st + 1] * 2
        tfull[lo * G:hi * G, :] = matmul(
            a_t[lo:hi].reshape((hi - lo) * G, s.F), thead[...], NT
        )
        for b in range(lo, hi):
            for r in range(X):
                tp[st][r, (b - lo) * per:(b - lo + 1) * per, :] = tfull[
                    b * G + r * per:b * G + (r + 1) * per, :
                ]
        for k in range(1, X):
            to = lax.rem(x - k + X, X)
            send(tp[st].at[to], tr[st].at[k], sem_ts.at[st, k], sem_tr.at[st, k], v, to)

    def gather(kinds):
        for kind in kinds:
            for ring in (0, 1):
                ring_wait(ring, kind)
                for later in next_kinds.get(kind, ()):
                    ring_send(ring, later)
                if kind != 6:
                    sib_send(ring, kind if kind < 6 else 6)
        for kind in kinds:
            for ring in (0, 1):
                if kind != 7:
                    sib_wait(ring, kind)

    for ring in (0, 1):
        sib_wait(ring, None)
    gather(first_kinds)
    target_stage(0)
    if Z == 8:
        gather((4, 5))
        target_stage(1)
        gather((6, 7))
        target_stage(2)

    load_d.wait()
    dp[...] = matmul(a_d[...].reshape(s.ROWS, s.F), dhead[...], NT).reshape(X, s.CH, s.VD)
    for k in range(1, X):
        send(dp.at[lax.rem(x - k + X, X)], dr.at[k], sem_ds.at[k], sem_dr.at[k], v,
             lax.rem(x - k + X, X))

    pieces = []
    for st in range(len(stages) - 1):
        for k in range(1, X):
            arrived(tr[st].at[k], sem_tr.at[st, k])
        piece = tp[st][x]
        for k in range(1, X):
            piece = piece + tr[st][k]
        pieces.append(piece)
    lt = jnp.concatenate(pieces, axis=0) if len(pieces) > 1 else pieces[0]
    live_limit = s.VT * V - s.VT // 2
    live = iota((1, s.VT), 1) + v * s.VT < live_limit
    tm = jnp.max(jnp.where(live, lt, FAR_BELOW), axis=1, keepdims=True)
    te = jnp.where(live, jnp.exp(lt - tm), 0.0)
    ts = jnp.sum(te, axis=1, keepdims=True)

    s_out[...] = jnp.zeros_like(s_out)

    lr, lz = R0.bit_length() - 1, Z.bit_length() - 1
    lx = zpx.bit_length() - 1

    def spot(src, dst):
        j_ = src & (R0 - 1)
        z_ = (src >> lr) & (zpx - 1)
        c_ = (src >> (lr + lx)) & 1
        c_ = c_ + c - 2 * c * c_
        i_ = src >> (lr + lx + 1)
        turn = jnp.zeros_like(src)
        for i, other in enumerate(turns):
            turn = jnp.where(i_ == i, other % Y, turn)
        y_ = (turn + y) & (Y - 1)
        return (((z_ * 2 + c_) * Y + y_) << lr) + j_ == dst

    eye = iota((s.CH, 128), 0) == iota((s.CH, 128), 1)
    eye_t = spot(iota((s.CH, 128), 0), iota((s.CH, 128), 1))

    def to_row(col, mask=eye):
        return jnp.sum(jnp.where(mask, col, 0.0), axis=0, keepdims=True)

    def to_col(row):
        return jnp.sum(jnp.where(eye, row, 0.0), axis=1, keepdims=True)

    @pl.when(owner)
    def _():
        te16 = te.astype(BF)
        square = (s.CH, s.CH)
        order = jnp.where(spot(iota(square, 1), iota(square, 0)), 1.0, 0.0).astype(BF)
        te16 = matmul(order, te16, NN).astype(BF)
        for i in range(2):
            s_out[i] = matmul(te16, sel[:, i * s.VD:(i + 1) * s.VD], NN).astype(BF)

    mass_here = jnp.sum(s_out[0].astype(F32) + s_out[1].astype(F32), axis=1, keepdims=True)
    tm_row, ts_row = to_row(tm, eye_t), to_row(ts, eye_t)
    st_own[...] = jnp.broadcast_to(tm_row, st_own.shape)

    def soft_copies(action):
        @pl.when(owner)
        def _():
            action(rcopy(s_out.at[1], s_in, sem_ss.at[1], sem_sr.at[0], 2 * v + 1, x))
            action(rcopy(st_own, st_in, sem_ss.at[3], sem_sr.at[1], 2 * v + 1, x))

            @pl.when(v > 0)
            def _():
                action(rcopy(s_out.at[0], s_in, sem_ss.at[0], sem_sr.at[0], 2 * v, x))
                action(rcopy(st_own, st_in, sem_ss.at[2], sem_sr.at[1], 2 * v, x))

    def soft_send():
        soft_copies(lambda cp: cp.start())
        drains.append(lambda: soft_copies(lambda cp: cp.wait_send()))

        @pl.when(v == 0)
        def _():
            s_in[...] = s_out[0]
            st_in[...] = st_own[...]

    soft_send()

    valid = dvalid[...] > 0
    for k in range(1, X):
        arrived(dr.at[k], sem_dr.at[k])
    l_d = dp[x]
    for k in range(1, X):
        l_d = l_d + dr[k]
    ld[...] = l_d
    dm = jnp.max(jnp.where(valid, l_d, FAR_BELOW), axis=1, keepdims=True)
    ds = jnp.sum(jnp.where(valid, jnp.exp(l_d - dm), 0.0), axis=1, keepdims=True)

    zero_row = jnp.zeros((5, 128), F32)
    maxes = jnp.concatenate([tm_row, tm_row, to_row(dm), zero_row], axis=0)
    sums = jnp.concatenate([ts_row, to_row(mass_here), to_row(ds), zero_row], axis=0)

    def exchange(buf, slot, n, peer, ssem, rsem):
        for k in range(1, n):
            send(buf.at[slot], buf.at[slot], ssem.at[k], rsem.at[k], peer(k))

    def exchange_wait(buf, slot, n, rsem):
        for k in range(1, n):
            arrived(buf.at[lax.rem(slot + n - k, n)], rsem.at[k])

    hops = (
        (f0, c0, c, 2, lambda k: sib),
        (f1, c1, y, Y, y_peer),
        (f2, c2, z, Z, z_peer),
    )
    for h, (buf, _, slot, n, peer) in enumerate(hops):
        buf[slot, 0] = maxes
        buf[slot, 1] = sums
        exchange(buf, slot, n, peer, sem_fs.at[h], sem_fr.at[h])
        exchange_wait(buf, slot, n, sem_fr.at[h])
        maxes = buf[0, 0]
        for i in range(1, n):
            maxes = jnp.maximum(maxes, buf[i, 0])
        sums = buf[0, 1] * jnp.exp(buf[0, 0] - maxes)
        for i in range(1, n):
            sums = sums + buf[i, 1] * jnp.exp(buf[i, 0] - maxes)

    @pl.when(v > 0)
    def _():
        arrived(s_in, sem_sr.at[0])
        arrived(st_in, sem_sr.at[1])

    t_max, t_total = maxes[0:1], sums[0:1]
    factor = to_col(jnp.exp(st_in[0:1] - t_max) / t_total)
    mass = to_col(sums[1:2] / t_total)
    lse = to_col(maxes[2:3] + jnp.log(sums[2:3]))
    soft = s_in[...].astype(F32) * factor
    l_d = ld[...]
    grad = scale[0, 0] * (jnp.exp(l_d - lse) * mass - soft)
    ga_t[pl.ds(x * s.SPC, s.SPC)] = (
        jnp.where(valid, grad, 0.0).astype(BF).reshape(s.SPC, G, s.VD)
    )
    for k in range(1, X):
        chunk = ga_t.at[pl.ds(x * s.SPC, s.SPC)]
        send(chunk, chunk, sem_gs.at[k], sem_gr.at[k], v, x_peer(k))

    cross = jnp.broadcast_to(to_row(jnp.sum(soft * l_d, axis=1, keepdims=True)), (8, 128))

    def cross_send(h, value):
        _, buf, slot, n, peer = hops[h]
        buf[slot] = value
        exchange(buf, slot, n, peer, sem_cs.at[h], sem_cr.at[h])

    def cross_wait(h):
        _, buf, slot, n, _ = hops[h]
        exchange_wait(buf, slot, n, sem_cr.at[h])
        total = buf[0]
        for i in range(1, n):
            total = total + buf[i]
        return total

    cross_send(0, cross)
    shape = (s.ROWS, s.ROWS)
    dpos, tpos = iota(shape, 0), iota(shape, 1)
    dj = dpos & (R0 - 1)
    dz = (dpos >> lr) & (Z - 1)
    dc = (dpos >> (lr + lz)) & 1
    dy = dpos >> (lr + lz + 1)
    perm = jnp.where((((dz * 2 + dc) * Y + dy) << lr) + dj == tpos, 1.0, 0.0).astype(BF)

    cross_send(1, cross_wait(0))

    for k in range(1, X):
        other = ga_t.at[pl.ds(lax.rem(x + X - k, X) * s.SPC, s.SPC)]
        arrived(other, sem_gr.at[k])
    ga_d[...] = (
        matmul(perm, ga_t[...].reshape(s.ROWS, s.VD), NN).astype(BF).reshape(2 * Y, G, s.VD)
    )

    def rows_of(buf, core):
        return jnp.concatenate([buf[i * 2 + core] for i in range(Z)], axis=0)

    js_t[...] = matmul(rows_of(ga_t, 1 - c), dhead[:, :H], NN).astype(BF).reshape(Z, G, H)
    send(js_t, jr_t, sem_js.at[0], sem_jr.at[0], sib)
    js_d[...] = matmul(rows_of(ga_d, 1 - c), dhead[:, H:], NN).astype(BF).reshape(Y, G, H)
    send(js_d, jr_d, sem_js.at[1], sem_jr.at[1], sib)
    keep_t[...] = matmul(rows_of(ga_t, c), dhead[:, :H], NN).reshape(Z, G, H)
    keep_d[...] = matmul(rows_of(ga_d, c), dhead[:, H:], NN).reshape(Y, G, H)

    parts = (
        (0, jr_t, keep_t, q_t, qr_t, z, Z, z_peer, y, Y, y_peer),
        (1, jr_d, keep_d, q_d, qr_d, y, Y, y_peer, z, Z, z_peer),
    )
    for i, jr, keep, q, qr, pos, n, peer, _, _, _ in parts:
        arrived(jr, sem_jr.at[i])
        for k in range(1, n):
            to = lax.rem(pos + k, n)
            q[k] = (keep[to] + jr[to].astype(F32)).astype(BF)
            send(q.at[k], qr.at[k], sem_qs.at[i, k], sem_qr.at[i, k], peer(k))

    ghead[...] = matmul(ga_t[...].reshape(s.ROWS, s.VD), a_d[...].reshape(s.ROWS, s.F), TN).astype(
        BF
    )
    store = pltpu.make_async_copy(ghead, ghead_out, sem_out)
    store.start()

    cross_send(2, cross_wait(1))

    for i, jr, keep, q, qr, pos, n, peer, pos2, n2, peer2 in parts:
        total = keep[pos] + jr[pos].astype(F32)
        for k in range(1, n):
            arrived(qr.at[k], sem_qr.at[i, k])
            total = total + qr[k].astype(F32)
        for k in range(nk):
            stage_big[0, pl.ds(k, G, stride=nk), :] = total[:, k * W2:(k + 1) * W2]
        for p in range(n2):
            w_out[i, p] = stage_big[0, p * G:(p + 1) * G, :].astype(BF)
        for k in range(1, n2):
            send(
                w_out.at[i, lax.rem(pos2 + k, n2)], w_in.at[i, k],
                sem_ws.at[i, k], sem_wr.at[i, k], peer2(k),
            )
        w_in[i, 0] = w_out[i, pos2]

    total_cross = to_col(cross_wait(2)[0:1])
    loss = mass * lse - total_cross
    shape = (s.CH, s.CH)
    src, dst = iota(shape, 0), iota(shape, 1)
    sj = src & (R0 - 1)
    sy = (src >> lr) & (Y - 1)
    sc = (src >> (lr + lz)) & 1
    sz = src >> (lr + lz + 1)
    place = (((sz * Y + sy) * 2 + sc) << lr) + sj == dst
    loss_out[...] = jnp.sum(jnp.where(place, loss, 0.0), axis=0, keepdims=True)

    for i, jr, keep, q, qr, pos, n, peer, pos2, n2, peer2 in parts:
        total = w_in[i, 0].astype(F32)
        for k in range(1, n2):
            arrived(w_in.at[i, k], sem_wr.at[i, k])
            total = total + w_in[i, k].astype(F32)
        stage[0] = total
        for k in range(nk):
            gh_out[:, i * H + k * W2:i * H + (k + 1) * W2] = stage[
                0, pl.ds(k, R0, stride=nk), :
            ].astype(BF)

    finish()
    store.wait()


def on_device(vocab, rows, th, thead, dh, dhead, dmap, dvalid, scale):
    s = Sizes(vocab, rows, th.shape, thead.shape, dhead.shape)
    Z, Y, X, G, F, H, W, W2, VT, VD, CH = (
        s.Z, s.Y, s.X, s.G, s.F, s.H, s.W, s.W2, s.VT, s.VD, s.CH
    )
    vm = pltpu.VMEM
    dma = pltpu.SemaphoreType.DMA
    stage_rows = (40, 16, 8) if Z == 8 else (CH, 8, 8)
    scratch = [
        vm((s.R0, F), BF), vm((s.R0, F), BF),
        vm((1, VD), jnp.int32), vm((1, VD), jnp.int32),
        vm((VT, F), BF), vm((VD, F), BF),
        vm((W // L, G, L), F32), vm((W // L, G * Y, L), F32),
        vm((Y, G, W), BF), vm((Z, G, W), BF),
        vm((2 * Z, G, F), BF), vm((2 * Y, G, F), BF),
        vm((8, VD), jnp.int32), vm((2, 8, VD), jnp.int32),
        vm((VT, 2 * VD), BF),
        *[vm((X, n, VT), F32) for n in stage_rows * 2],
        vm((s.ROWS, VT), F32),
        vm((X, CH, VD), F32), vm((X, CH, VD), F32),
        vm((CH, VD), F32),
        vm((2, CH, VD), BF), vm((CH, VD), BF),
        vm((8, 128), F32), vm((8, 128), F32),
        vm((2, 2, 8, 128), F32), vm((Y, 2, 8, 128), F32), vm((Z, 2, 8, 128), F32),
        vm((2, 8, 128), F32), vm((Y, 8, 128), F32), vm((Z, 8, 128), F32),
        vm((2 * Z, G, VD), BF), vm((2 * Y, G, VD), BF),
        vm((Z, G, H), F32), vm((Y, G, H), F32),
        vm((Z, G, H), BF), vm((Y, G, H), BF),
        vm((Z, G, H), BF), vm((Y, G, H), BF),
        vm((Z, G, H), BF), vm((Y, G, H), BF),
        vm((Z, G, H), BF), vm((Y, G, H), BF),
        vm((2, Y, G, W2), BF), vm((2, Y, G, W2), BF),
        vm((VD, F), BF),
        dma((6,)),
        dma((2, Y)), dma((2, Y)),
        dma((2, 8)), dma((2, 8)),
        dma((2, 8)), dma((2, 8)),
        dma, dma((2,)),
        dma((3, X)), dma((3, X)), dma((X,)), dma((X,)),
        dma((4,)), dma((2,)),
        dma((3, Z)), dma((3, Z)), dma((3, Z)), dma((3, Z)),
        dma((X,)), dma((X,)),
        dma((2,)), dma((2,)), dma((2, Z)), dma((2, Z)), dma((2, Z)), dma((2, Z)),
        dma,
    ]
    hbm = pl.BlockSpec(memory_space=pltpu.HBM)
    vmem = pl.BlockSpec(memory_space=pltpu.VMEM)
    smem = pl.BlockSpec(memory_space=pltpu.SMEM)
    loss, gh, ghead = pl.pallas_call(
        functools.partial(body, s),
        out_shape=(
            jax.ShapeDtypeStruct((1, CH), F32),
            jax.ShapeDtypeStruct((s.R0, F), BF),
            jax.ShapeDtypeStruct((VD, F), BF),
        ),
        in_specs=[hbm, hbm, hbm, hbm, hbm, hbm, smem],
        out_specs=(vmem, vmem, hbm),
        scratch_shapes=scratch,
        compiler_params=pltpu.CompilerParams(
            collective_id=0, has_side_effects=True, vmem_limit_bytes=63 * 1024 * 1024
        ),
    )(th, dh, thead, dhead, dmap.reshape(1, VD), dvalid.reshape(1, VD), scale.reshape(1, 1))
    return hand_out(ghead, gh, loss)


def hand_out(*arrays):
    def copy(*refs):
        n = len(arrays)
        held, sems = refs[2 * n:3 * n], refs[3 * n]
        moves = []
        for src, mid, dst in zip(refs[:n], held, refs[n:2 * n]):
            rows = src.shape[0]
            cut = rows // 4 if rows >= 128 else rows
            for i in range(0, rows, cut):
                part = pl.ds(i, cut)
                k = len(moves)
                moves.append((
                    pltpu.make_async_copy(src.at[part], mid.at[part], sems.at[0, k]),
                    pltpu.make_async_copy(mid.at[part], dst.at[part], sems.at[1, k]),
                ))
        for come, _ in moves:
            come.start()
        for come, go in moves:
            come.wait()
            go.start()
        for _, go in moves:
            go.wait()

    hbm = pl.BlockSpec(memory_space=pltpu.HBM)
    ghead, gh, loss = pl.pallas_call(
        copy,
        out_shape=tuple(jax.ShapeDtypeStruct(a.shape, a.dtype) for a in arrays),
        in_specs=[hbm] * len(arrays),
        out_specs=(hbm,) * len(arrays),
        scratch_shapes=[
            *[pltpu.VMEM(a.shape, a.dtype) for a in arrays],
            pltpu.SemaphoreType.DMA((2, 8)),
        ],
        compiler_params=pltpu.CompilerParams(vmem_limit_bytes=63 * 1024 * 1024),
    )(*arrays)
    return loss.reshape(loss.shape[1]), gh, ghead


def solution(mesh):
    both, one = P("vocab", "rows"), P("vocab")
    return jax.shard_map(
        functools.partial(on_device, mesh.shape["vocab"], mesh.shape["rows"]),
        mesh=mesh,
        in_specs=(both, both, both, both, one, one, P()),
        out_specs=(P("rows"), both, both),
        check_vma=False,
    )
```

```python
import functools
import math

import jax
import jax.numpy as jnp
from jax import lax
from jax.experimental import pallas as pl
from jax.experimental.pallas import tpu as pltpu
from jax.sharding import PartitionSpec as P

MESH = pl.DeviceIdType.MESH
FAR_BELOW = -1e30
L = 128
NT = (((1,), (1,)), ((), ()))
TN = (((0,), (0,)), ((), ()))
NN = (((1,), (0,)), ((), ()))
BF = jnp.bfloat16
F32 = jnp.float32


def matmul(a, b, dims):
    return lax.dot_general(a, b, dims, preferred_element_type=F32)


def iota(shape, dim):
    return lax.broadcasted_iota(jnp.int32, shape, dim)


def far_first(n):
    return sorted(range(1, n), key=lambda k: -min(k, n - k))


class Sizes:
    def __init__(self, vocab, rows, th, thead, dhead):
        self.V, self.X = vocab, rows
        self.Z = self.Y = math.isqrt(vocab // 2)
        self.R0, self.F = th
        self.G = self.R0 * self.Z
        self.nk = self.G // self.R0
        self.W = self.F // self.nk
        self.H = self.F // 2
        self.W2 = self.H // self.nk
        self.VT, self.VD = thead[0], dhead[0]
        self.ROWS = self.R0 * vocab
        self.CH = self.ROWS // rows
        self.SPC = self.CH // self.G


def body(
    s,
    th_hbm, dh_hbm, thead_hbm, dhead_hbm, dmap_hbm, dvalid_hbm, scale,
    loss_out, gh_out, ghead_out,
    th, dh, dmap, dvalid, thead, dhead, stage, stage_big, t0, d0, a_t, a_d, map_own, map_in, sel, used,
    tp0, tp1, tp2, tr0, tr1, tr2, tfull, dp, dr, ld, s_out, s_in, st_own, st_in, f1, f2, c1, c2,
    ga_t, ga_d, keep_t, keep_d, js_t, js_d, jr_t, jr_d, q_t, q_d, qr_t, qr_d,
    w_out, w_in, ghead,
    sem_head, sem_l1s, sem_l1r, sem_rs, sem_rr, sem_sibs, sem_sibr, sem_ms, sem_mr,
    sem_ts, sem_tr, sem_ds, sem_dr, sem_ss, sem_sr, sem_fs, sem_fr, sem_cs, sem_cr,
    sem_gs, sem_gr, sem_js, sem_jr, sem_qs, sem_qr, sem_ws, sem_wr, sem_out,
):
    V, X, Z, Y, R0, G, nk, W, H, W2 = s.V, s.X, s.Z, s.Y, s.R0, s.G, s.nk, s.W, s.H, s.W2
    v = lax.axis_index("vocab")
    x = lax.axis_index("rows")
    c = lax.rem(v, 2)
    chip = lax.div(v, 2)
    y = lax.rem(chip, Y)
    z = lax.div(chip, Y)
    sib = v + 1 - 2 * c

    def at(zz, yy, cc):
        return (zz * Y + yy) * 2 + cc

    def y_peer(k):
        return at(z, lax.rem(y + k, Y), c)

    def z_peer(k):
        return at(lax.rem(z + k, Z), y, c)

    def x_peer(k):
        return lax.rem(x + k, X)

    def rcopy(src, dst, ssem, rsem, vv, xx):
        return pltpu.make_async_remote_copy(
            src_ref=src, dst_ref=dst, send_sem=ssem, recv_sem=rsem,
            device_id=(vv, xx), device_id_type=MESH,
        )

    tp, tr = (tp0, tp1, tp2), (tr0, tr1, tr2)
    sends = []
    drains = []

    def send(src, dst, ssem, rsem, vv, xx=None):
        cp = rcopy(src, dst, ssem, rsem, vv, x if xx is None else xx)
        cp.start()
        sends.append(cp)

    def arrived(dst, rsem):
        rcopy(dst, dst, rsem, rsem, sib, x).wait_recv()

    def finish():
        for cp in sends:
            cp.wait_send()
        for drain in drains:
            drain()

    owner = v < V // 2
    owner_of = lax.div(v, 2)

    barrier = pltpu.get_barrier_semaphore()

    def hello(vv, xx):
        pl.semaphore_signal(barrier, inc=1, device_id=(vv, xx), device_id_type=MESH)

    @pl.when(v > 0)
    def _():
        hello(owner_of, x)

    @pl.when(owner)
    def _():
        hello(2 * v + 1, x)

    @pl.when(jnp.logical_and(owner, v > 0))
    def _():
        hello(2 * v, x)

    for k in far_first(Y):
        for core in (0, 1):
            hello(at(z, lax.rem(y + k, Y), core), x)
    for k in far_first(Z):
        hello(z_peer(k), x)
    hello(sib, x)
    for k in range(1, X):
        hello(v, x_peer(k))

    small = [
        pltpu.make_async_copy(src, dst, sem_head.at[2 + i])
        for i, (src, dst) in enumerate(
            ((th_hbm, th), (dh_hbm, dh), (dmap_hbm, dmap), (dvalid_hbm, dvalid))
        )
    ]
    for cp in small:
        cp.start()
    load_t = pltpu.make_async_copy(thead_hbm, thead, sem_head.at[0])
    load_d = pltpu.make_async_copy(dhead_hbm, dhead, sem_head.at[1])
    load_t.start()
    load_d.start()

    for cp in small:
        cp.wait()

    for ref, dst, slot in ((th, t0, z), (dh, d0, y)):
        for k in range(nk):
            for a in range(W // L):
                cols = slice(k * W + a * L, k * W + (a + 1) * L)
                stage[a, pl.ds(k, R0, stride=nk), :] = ref[:, cols].astype(F32)
        for a in range(W // L):
            dst[slot, :, a * L:(a + 1) * L] = stage[a].astype(BF)
    masked_map = jnp.where(dvalid[...] > 0, dmap[...], -1)
    map_own[...] = jnp.broadcast_to(masked_map, map_own.shape)

    live_owner = owner.astype(jnp.int32)
    live_v = (v > 0).astype(jnp.int32)
    pl.semaphore_wait(
        barrier, 2 * (Y - 1) + (Z - 1) + 1 + (X - 1) + live_v + live_owner * (1 + live_v)
    )

    for k in far_first(Z):
        send(t0.at[z], t0.at[z], sem_l1s.at[0, k], sem_l1r.at[0, k], z_peer(k))
        send(d0.at[y], d0.at[y], sem_l1s.at[1, k], sem_l1r.at[1, k], y_peer(k))

    @pl.when(v > 0)
    def _():
        rcopy(map_own, map_in.at[c], sem_ms, sem_mr.at[c], owner_of, x).start()

    def drain_map():
        @pl.when(v > 0)
        def _():
            rcopy(map_own, map_in.at[c], sem_ms, sem_mr.at[c], owner_of, x).wait_send()

    drains.append(drain_map)

    @pl.when(v == 0)
    def _():
        map_in[0] = map_own[...]

    def relayout(src, dst, slot):
        for i in range(Y):
            for a in range(W // L):
                stage_big[a, i * G:(i + 1) * G, :] = src[i, :, a * L:(a + 1) * L].astype(F32)
        for k in range(nk):
            for a in range(W // L):
                cols = slice(k * W + a * L, k * W + (a + 1) * L)
                dst[slot, :, cols] = stage_big[a, pl.ds(k, G, stride=nk), :].astype(BF)

    for k in range(1, Z):
        arrived(t0.at[lax.rem(z + Z - k, Z)], sem_l1r.at[0, k])
    relayout(t0, a_t, 0)

    hop = (2, -2, 1, -1, 1, -1, 2, -2)
    held = (0, 0, 0, 0, -2, 2, -2, 2)
    if Z == 8:
        first_kinds, next_kinds = (0, 1, 2, 3), {0: (4, 6), 1: (5, 7)}
        turns, stages = (0, -2, 2, -1, 1, -3, 3, 4), (0, 5, 7, 8)
    else:
        first_kinds, next_kinds = (2,), {}
        turns, stages = (0, 1), (0, 2)

    def turn_slot(ring, turn, core):
        if ring == 1:
            return lax.rem(z + turn + Z, Z) * 2 + core
        near = [i for i, other in enumerate(turns) if (other - turn) % Y == 0]
        return near[0] * 2 + (0 if core is c else 1)

    def block_of(ring, turn, kind, core):
        buf, slot = (a_t, a_d)[ring], turn_slot(ring, turn, core)
        if kind is None or kind < 6:
            return buf.at[slot]
        return buf.at[slot, :, pl.ds(0, H)] if kind == 6 else buf.at[slot, :, pl.ds(H, H)]

    def ring_send(ring, kind):
        src = block_of(ring, held[kind], kind, c)
        dst = src if ring == 1 else block_of(ring, held[kind] - hop[kind], kind, c)
        send(src, dst, sem_rs.at[ring, kind], sem_rr.at[ring, kind],
             (y_peer, z_peer)[ring](hop[kind] % Z))

    def ring_wait(ring, kind):
        arrived(block_of(ring, held[kind] - hop[kind], kind, c), sem_rr.at[ring, kind])

    def sib_turn(kind):
        return 0 if kind is None else held[kind] - hop[kind]

    def sib_send(ring, kind):
        turn, k = sib_turn(kind), 7 if kind is None else kind
        src = block_of(ring, turn, None, c)
        dst = src if ring == 1 else block_of(ring, turn, None, 1 - c)
        send(src, dst, sem_sibs.at[ring, k], sem_sibr.at[ring, k], sib)

    def sib_wait(ring, kind):
        k = 7 if kind is None else kind
        arrived(block_of(ring, sib_turn(kind), None, 1 - c), sem_sibr.at[ring, k])

    def ring_start(ring):
        for kind in first_kinds:
            ring_send(ring, kind)
        sib_send(ring, None)

    ring_start(0)
    for k in range(1, Y):
        arrived(d0.at[lax.rem(y + Y - k, Y)], sem_l1r.at[1, k])
    relayout(d0, a_d, z * 2 + c)
    ring_start(1)

    used[...] = jnp.zeros_like(used)

    @pl.when(owner)
    def _():
        arrived(map_in.at[1], sem_mr.at[1])

        @pl.when(v > 0)
        def _():
            arrived(map_in.at[0], sem_mr.at[0])

        ids = iota((s.VT, s.VD), 0) + v * s.VT
        for i in range(2):
            hit = ids == jnp.broadcast_to(map_in[i, 0:1, :], (s.VT, s.VD))
            sel[:, i * s.VD:(i + 1) * s.VD] = jnp.where(hit, 1.0, 0.0).astype(BF)
        used[...] = matmul(jnp.ones((8, 2 * s.VD), BF), sel[...], NT)

    load_t.wait()

    zpx = Z // X
    per = zpx * R0

    def target_stage(st):
        lo, hi = stages[st] * 2, stages[st + 1] * 2
        tfull[lo * G:hi * G, :] = matmul(
            a_t[lo:hi].reshape((hi - lo) * G, s.F), thead[...], NT
        )
        for b in range(lo, hi):
            for r in range(X):
                tp[st][r, (b - lo) * per:(b - lo + 1) * per, :] = tfull[
                    b * G + r * per:b * G + (r + 1) * per, :
                ]
        for k in range(1, X):
            to = lax.rem(x - k + X, X)
            send(tp[st].at[to], tr[st].at[k], sem_ts.at[st, k], sem_tr.at[st, k], v, to)

    def gather(kinds):
        for kind in kinds:
            for ring in (0, 1):
                ring_wait(ring, kind)
                for later in next_kinds.get(kind, ()):
                    ring_send(ring, later)
                if kind != 6:
                    sib_send(ring, kind if kind < 6 else 6)
        for kind in kinds:
            for ring in (0, 1):
                if kind != 7:
                    sib_wait(ring, kind)

    def draft_rows():
        whole = matmul(a_d[...].reshape(s.ROWS, s.F), dhead[...], NT)
        for zz in range(Z):
            dp[zz] = whole[zz * 2 * G:(zz + 1) * 2 * G]
        for k in range(1, X):
            to = lax.rem(x - k + X, X)
            for i in range(zpx):
                send(dp.at[to * zpx + i], dr.at[k, i], sem_ds.at[k, i], sem_dr.at[k, i], v, to)

    for ring in (0, 1):
        sib_wait(ring, None)
    gather(first_kinds)
    target_stage(0)
    load_d.wait()
    if Z == 8:
        gather((4, 5))
        target_stage(1)
        gather((6, 7))
        target_stage(2)
    draft_rows()

    live_limit = s.VT * V - s.VT // 2
    live = iota((1, s.VT), 1) + v * s.VT < live_limit
    by_stage = []
    for st in range(len(stages) - 1):
        for k in range(1, X):
            arrived(tr[st].at[k], sem_tr.at[st, k])
        lt = tp[st][x]
        for k in range(1, X):
            lt = lt + tr[st][k]
        high = jnp.max(jnp.where(live, lt, FAR_BELOW), axis=1, keepdims=True)
        grown = jnp.where(live, jnp.exp(lt - high), 0.0)
        rounded = grown.astype(BF).astype(F32)
        by_stage.append((
            high, jnp.sum(grown, axis=1, keepdims=True), rounded,
            jnp.sum(rounded * used[0:1], axis=1, keepdims=True),
        ))
    tm, ts, te, mass_here = (
        jnp.concatenate(cols, axis=0) if len(cols) > 1 else cols[0] for cols in zip(*by_stage)
    )

    lr, lz = R0.bit_length() - 1, Z.bit_length() - 1
    lx = zpx.bit_length() - 1

    def spot(src, dst):
        j_ = src & (R0 - 1)
        z_ = (src >> lr) & (zpx - 1)
        c_ = (src >> (lr + lx)) & 1
        c_ = c_ + c - 2 * c * c_
        i_ = src >> (lr + lx + 1)
        turn = jnp.zeros_like(src)
        for i, other in enumerate(turns):
            turn = jnp.where(i_ == i, other % Y, turn)
        y_ = (turn + y) & (Y - 1)
        return (((z_ * 2 + c_) * Y + y_) << lr) + j_ == dst

    eye = iota((s.CH, 128), 0) == iota((s.CH, 128), 1)
    eye_t = spot(iota((s.CH, 128), 0), iota((s.CH, 128), 1))

    def to_row(col, mask=eye):
        return jnp.sum(jnp.where(mask, col, 0.0), axis=0, keepdims=True)

    eye_hi = iota((s.CH, 128), 0) + 64 == iota((s.CH, 128), 1)

    def to_col(row, mask=eye):
        return jnp.sum(jnp.where(mask, row, 0.0), axis=1, keepdims=True)

    te16 = te.astype(BF)
    tm_row, ts_row = to_row(tm, eye_t), to_row(ts, eye_t)
    st_own[...] = tm_row

    @pl.when(owner)
    def _():
        square = (s.CH, s.CH)
        order = jnp.where(spot(iota(square, 1), iota(square, 0)), 1.0, 0.0).astype(BF)
        rows = matmul(order, te16, NN).astype(BF)
        for i in range(2):
            s_out[i] = matmul(rows, sel[:, i * s.VD:(i + 1) * s.VD], NN).astype(BF)

    def soft_copies(action):
        @pl.when(owner)
        def _():
            action(rcopy(s_out.at[1], s_in, sem_ss.at[1], sem_sr.at[0], 2 * v + 1, x))
            action(rcopy(st_own, st_in, sem_ss.at[3], sem_sr.at[1], 2 * v + 1, x))

            @pl.when(v > 0)
            def _():
                action(rcopy(s_out.at[0], s_in, sem_ss.at[0], sem_sr.at[0], 2 * v, x))
                action(rcopy(st_own, st_in, sem_ss.at[2], sem_sr.at[1], 2 * v, x))

    def soft_send():
        soft_copies(lambda cp: cp.start())
        drains.append(lambda: soft_copies(lambda cp: cp.wait_send()))

        @pl.when(v == 0)
        def _():
            s_in[...] = s_out[0]
            st_in[...] = st_own[...]

    soft_send()

    valid = dvalid[...] > 0
    blocks = []
    for i in range(zpx):
        block = dp[x * zpx + i]
        for k in range(1, X):
            arrived(dr.at[k, i], sem_dr.at[k, i])
            block = block + dr[k, i]
        blocks.append(block)
    l_d = jnp.concatenate(blocks, axis=0) if zpx > 1 else blocks[0]
    ld[...] = l_d
    dm = jnp.max(jnp.where(valid, l_d, FAR_BELOW), axis=1, keepdims=True)
    ds = jnp.sum(jnp.where(valid, jnp.exp(l_d - dm), 0.0), axis=1, keepdims=True)

    maxes = tm_row + to_row(dm, eye_hi)
    sums = ts_row + to_row(ds, eye_hi)
    masses = to_row(mass_here, eye_t)

    def all_of_y():
        own_slot = y * 2 + c
        out = [
            (at(z, lax.rem(y + k, Y), core), 2 * k + core, 2 * k + c)
            for k in far_first(Y) for core in (0, 1)
        ] + [(sib, 0, c)]
        came = [(sib - at(z, 0, 0), 1 - c)] + [
            (lax.rem(y + Y - k, Y) * 2 + core, 2 * k + core)
            for k in far_first(Y)[::-1] for core in (0, 1)
        ]
        return own_slot, 2 * Y, out, came

    def all_of_z():
        out = [(z_peer(k), k, k) for k in far_first(Z)]
        came = [(lax.rem(z + Z - k, Z), k) for k in far_first(Z)[::-1]]
        return z, Z, out, came

    hops = (all_of_y(), all_of_z())

    def exchange(h, bufs, ssem, rsem, value):
        own_slot, _, out, _ = hops[h]
        bufs[h][own_slot] = value
        for to, i, k in out:
            ref = bufs[h].at[own_slot]
            send(ref, ref, ssem.at[h, i], rsem.at[h, k], to)

    def exchange_wait(h, bufs, rsem):
        for slot, k in hops[h][3]:
            arrived(bufs[h].at[slot], rsem.at[h, k])

    stats = (f1, f2)
    exchange(0, stats, sem_fs, sem_fr, jnp.concatenate([maxes, sums, masses], axis=1))

    for h in range(2):
        buf, n = stats[h], hops[h][1]
        exchange_wait(h, stats, sem_fr)
        maxes = buf[0, :, 0:L]
        for i in range(1, n):
            maxes = jnp.maximum(maxes, buf[i, :, 0:L])
        sums, masses = jnp.zeros_like(maxes), jnp.zeros_like(maxes)
        for i in range(n):
            share = jnp.exp(buf[i, :, 0:L] - maxes)
            sums = sums + buf[i, :, L:2 * L] * share
            masses = masses + buf[i, :, 2 * L:3 * L] * share
        if h == 0:
            exchange(1, stats, sem_fs, sem_fr, jnp.concatenate([maxes, sums, masses], axis=1))

    @pl.when(v > 0)
    def _():
        arrived(s_in, sem_sr.at[0])
        arrived(st_in, sem_sr.at[1])

    t_total = to_col(sums)
    factor = jnp.exp(to_col(st_in[...]) - to_col(maxes)) / t_total
    mass = to_col(masses) / t_total
    lse = to_col(maxes, eye_hi) + jnp.log(to_col(sums, eye_hi))
    soft = s_in[...].astype(F32) * factor
    l_d = ld[...]
    grad = scale[0, 0] * (jnp.exp(l_d - lse) * mass - soft)
    ga_t[pl.ds(x * s.SPC, s.SPC)] = (
        jnp.where(valid, grad, 0.0).astype(BF).reshape(s.SPC, G, s.VD)
    )
    for k in range(1, X):
        chunk = ga_t.at[pl.ds(x * s.SPC, s.SPC)]
        send(chunk, chunk, sem_gs.at[k], sem_gr.at[k], v, x_peer(k))

    cross = to_row(jnp.sum(soft * l_d, axis=1, keepdims=True))

    cross_bufs = (c1, c2)

    def cross_send(h, value):
        exchange(h, cross_bufs, sem_cs, sem_cr, value)

    def cross_wait(h):
        exchange_wait(h, cross_bufs, sem_cr)
        total = cross_bufs[h][0]
        for i in range(1, hops[h][1]):
            total = total + cross_bufs[h][i]
        return total

    cross_send(0, cross)
    shape = (s.ROWS, s.ROWS)
    dpos, tpos = iota(shape, 0), iota(shape, 1)
    dj = dpos & (R0 - 1)
    dz = (dpos >> lr) & (Z - 1)
    dc = (dpos >> (lr + lz)) & 1
    dy = dpos >> (lr + lz + 1)
    perm = jnp.where((((dz * 2 + dc) * Y + dy) << lr) + dj == tpos, 1.0, 0.0).astype(BF)

    for k in range(1, X):
        other = ga_t.at[pl.ds(lax.rem(x + X - k, X) * s.SPC, s.SPC)]
        arrived(other, sem_gr.at[k])
    def rows_of(buf, core):
        return jnp.concatenate([buf[i * 2 + core] for i in range(Z)], axis=0)

    js_t[...] = matmul(rows_of(ga_t, 1 - c), dhead[:, :H], NN).astype(BF).reshape(Z, G, H)
    send(js_t, jr_t, sem_js.at[0], sem_jr.at[0], sib)
    ga_d[...] = (
        matmul(perm, ga_t[...].reshape(s.ROWS, s.VD), NN).astype(BF).reshape(2 * Y, G, s.VD)
    )
    js_d[...] = matmul(rows_of(ga_d, 1 - c), dhead[:, H:], NN).astype(BF).reshape(Y, G, H)
    send(js_d, jr_d, sem_js.at[1], sem_jr.at[1], sib)
    keep_t[...] = matmul(rows_of(ga_t, c), dhead[:, :H], NN).reshape(Z, G, H)
    keep_d[...] = matmul(rows_of(ga_d, c), dhead[:, H:], NN).reshape(Y, G, H)

    parts = (
        (0, jr_t, keep_t, q_t, qr_t, z, Z, z_peer, y, Y, y_peer),
        (1, jr_d, keep_d, q_d, qr_d, y, Y, y_peer, z, Z, z_peer),
    )
    for i, jr, *_ in parts:
        arrived(jr, sem_jr.at[i])
    for k in far_first(Z):
        for i, jr, keep, q, qr, pos, n, peer, _, _, _ in parts:
            to = lax.rem(pos + k, n)
            q[k] = (keep[to] + jr[to].astype(F32)).astype(BF)
            send(q.at[k], qr.at[k], sem_qs.at[i, k], sem_qr.at[i, k], peer(k))

    ghead[...] = matmul(ga_t[...].reshape(s.ROWS, s.VD), a_d[...].reshape(s.ROWS, s.F), TN).astype(
        BF
    )
    store = pltpu.make_async_copy(ghead, ghead_out, sem_out)
    store.start()

    cross_send(1, cross_wait(0))

    for i, jr, keep, q, qr, pos, n, peer, pos2, n2, peer2 in parts:
        total = keep[pos] + jr[pos].astype(F32)
        for k in far_first(n)[::-1]:
            arrived(qr.at[k], sem_qr.at[i, k])
            total = total + qr[k].astype(F32)
        for k in range(nk):
            stage_big[0, pl.ds(k, G, stride=nk), :] = total[:, k * W2:(k + 1) * W2]
        for p in range(n2):
            w_out[i, p] = stage_big[0, p * G:(p + 1) * G, :].astype(BF)
        for k in far_first(n2):
            send(
                w_out.at[i, lax.rem(pos2 + k, n2)], w_in.at[i, k],
                sem_ws.at[i, k], sem_wr.at[i, k], peer2(k),
            )
        w_in[i, 0] = w_out[i, pos2]

    total_cross = to_col(cross_wait(1))
    loss = mass * lse - total_cross
    shape = (s.CH, s.CH)
    src, dst = iota(shape, 0), iota(shape, 1)
    sj = src & (R0 - 1)
    sy = (src >> lr) & (Y - 1)
    sc = (src >> (lr + lz)) & 1
    sz = src >> (lr + lz + 1)
    place = (((sz * Y + sy) * 2 + sc) << lr) + sj == dst
    loss_out[...] = jnp.sum(jnp.where(place, loss, 0.0), axis=0, keepdims=True)

    for i, jr, keep, q, qr, pos, n, peer, pos2, n2, peer2 in parts:
        total = w_in[i, 0].astype(F32)
        for k in range(1, n2):
            arrived(w_in.at[i, k], sem_wr.at[i, k])
            total = total + w_in[i, k].astype(F32)
        stage[0] = total
        for k in range(nk):
            gh_out[:, i * H + k * W2:i * H + (k + 1) * W2] = stage[
                0, pl.ds(k, R0, stride=nk), :
            ].astype(BF)

    finish()
    store.wait()


def on_device(vocab, rows, th, thead, dh, dhead, dmap, dvalid, scale):
    s = Sizes(vocab, rows, th.shape, thead.shape, dhead.shape)
    Z, Y, X, G, F, H, W, W2, VT, VD, CH = (
        s.Z, s.Y, s.X, s.G, s.F, s.H, s.W, s.W2, s.VT, s.VD, s.CH
    )
    vm = pltpu.VMEM
    dma = pltpu.SemaphoreType.DMA
    stage_rows = (40, 16, 8) if Z == 8 else (CH, 8, 8)
    scratch = [
        vm((s.R0, F), BF), vm((s.R0, F), BF),
        vm((1, VD), jnp.int32), vm((1, VD), jnp.int32),
        vm((VT, F), BF), vm((VD, F), BF),
        vm((W // L, G, L), F32), vm((W // L, G * Y, L), F32),
        vm((Y, G, W), BF), vm((Z, G, W), BF),
        vm((2 * Z, G, F), BF), vm((2 * Y, G, F), BF),
        vm((8, VD), jnp.int32), vm((2, 8, VD), jnp.int32),
        vm((VT, 2 * VD), BF), vm((8, VT), F32),
        *[vm((X, n, VT), F32) for n in stage_rows * 2],
        vm((s.ROWS, VT), F32),
        vm((Z, 2 * G, VD), F32), vm((X, Z // X, 2 * G, VD), F32),
        vm((CH, VD), F32),
        vm((2, CH, VD), BF), vm((CH, VD), BF),
        vm((1, 128), F32), vm((1, 128), F32),
        vm((2 * Y, 1, 3 * L), F32), vm((Z, 1, 3 * L), F32),
        vm((2 * Y, 1, L), F32), vm((Z, 1, L), F32),
        vm((2 * Z, G, VD), BF), vm((2 * Y, G, VD), BF),
        vm((Z, G, H), F32), vm((Y, G, H), F32),
        vm((Z, G, H), BF), vm((Y, G, H), BF),
        vm((Z, G, H), BF), vm((Y, G, H), BF),
        vm((Z, G, H), BF), vm((Y, G, H), BF),
        vm((Z, G, H), BF), vm((Y, G, H), BF),
        vm((2, Y, G, W2), BF), vm((2, Y, G, W2), BF),
        vm((VD, F), BF),
        dma((6,)),
        dma((2, Y)), dma((2, Y)),
        dma((2, 8)), dma((2, 8)),
        dma((2, 8)), dma((2, 8)),
        dma, dma((2,)),
        dma((3, X)), dma((3, X)), dma((X, Z // X)), dma((X, Z // X)),
        dma((4,)), dma((2,)),
        *[dma((2, 2 * Y))] * 4,
        dma((X,)), dma((X,)),
        dma((2,)), dma((2,)), dma((2, Z)), dma((2, Z)), dma((2, Z)), dma((2, Z)),
        dma,
    ]
    hbm = pl.BlockSpec(memory_space=pltpu.HBM)
    vmem = pl.BlockSpec(memory_space=pltpu.VMEM)
    smem = pl.BlockSpec(memory_space=pltpu.SMEM)
    loss, gh, ghead = pl.pallas_call(
        functools.partial(body, s),
        out_shape=(
            jax.ShapeDtypeStruct((1, CH), F32),
            jax.ShapeDtypeStruct((s.R0, F), BF),
            jax.ShapeDtypeStruct((VD, F), BF),
        ),
        in_specs=[hbm, hbm, hbm, hbm, hbm, hbm, smem],
        out_specs=(vmem, vmem, hbm),
        scratch_shapes=scratch,
        compiler_params=pltpu.CompilerParams(
            collective_id=0, has_side_effects=True, vmem_limit_bytes=63 * 1024 * 1024
        ),
    )(th, dh, thead, dhead, dmap.reshape(1, VD), dvalid.reshape(1, VD), scale.reshape(1, 1))
    return hand_out(ghead, gh, loss)


def hand_out(*arrays):
    def copy(*refs):
        n = len(arrays)
        held, sems = refs[2 * n:3 * n], refs[3 * n]
        moves = []
        for src, mid, dst in zip(refs[:n], held, refs[n:2 * n]):
            rows = src.shape[0]
            cut = rows // 4 if rows >= 128 else rows
            for i in range(0, rows, cut):
                part = pl.ds(i, cut)
                k = len(moves)
                moves.append((
                    pltpu.make_async_copy(src.at[part], mid.at[part], sems.at[0, k]),
                    pltpu.make_async_copy(mid.at[part], dst.at[part], sems.at[1, k]),
                ))
        for come, _ in moves:
            come.start()
        for come, go in moves:
            come.wait()
            go.start()
        for _, go in moves:
            go.wait()

    hbm = pl.BlockSpec(memory_space=pltpu.HBM)
    ghead, gh, loss = pl.pallas_call(
        copy,
        out_shape=tuple(jax.ShapeDtypeStruct(a.shape, a.dtype) for a in arrays),
        in_specs=[hbm] * len(arrays),
        out_specs=(hbm,) * len(arrays),
        scratch_shapes=[
            *[pltpu.VMEM(a.shape, a.dtype) for a in arrays],
            pltpu.SemaphoreType.DMA((2, 8)),
        ],
        compiler_params=pltpu.CompilerParams(vmem_limit_bytes=63 * 1024 * 1024),
    )(*arrays)
    return loss.reshape(loss.shape[1]), gh, ghead


def solution(mesh):
    both, one = P("vocab", "rows"), P("vocab")
    return jax.shard_map(
        functools.partial(on_device, mesh.shape["vocab"], mesh.shape["rows"]),
        mesh=mesh,
        in_specs=(both, both, both, both, one, one, P()),
        out_specs=(P("rows"), both, both),
        check_vma=False,
    )
```

```python
import functools
import math

import jax
import jax.numpy as jnp
from jax import lax
from jax.experimental import pallas as pl
from jax.experimental.pallas import tpu as pltpu
from jax.sharding import PartitionSpec as P

MESH = pl.DeviceIdType.MESH
FAR_BELOW = -1e30
L = 128
NT = (((1,), (1,)), ((), ()))
TN = (((0,), (0,)), ((), ()))
NN = (((1,), (0,)), ((), ()))
BF = jnp.bfloat16
F32 = jnp.float32


def matmul(a, b, dims):
    return lax.dot_general(a, b, dims, preferred_element_type=F32)


def iota(shape, dim):
    return lax.broadcasted_iota(jnp.int32, shape, dim)


def far_first(n):
    return sorted(range(1, n), key=lambda k: -min(k, n - k))


class Sizes:
    def __init__(self, vocab, rows, th, thead, dhead):
        self.V, self.X = vocab, rows
        self.Z = self.Y = math.isqrt(vocab // 2)
        self.R0, self.F = th
        self.G = self.R0 * self.Z
        self.nk = self.G // self.R0
        self.W = self.F // self.nk
        self.H = self.F // 2
        self.W2 = self.H // self.nk
        self.VT, self.VD = thead[0], dhead[0]
        self.ROWS = self.R0 * vocab
        self.CH = self.ROWS // rows
        self.SPC = self.CH // self.G


def body(
    s,
    th_hbm, dh_hbm, thead_hbm, dhead_hbm, dmap_hbm, dvalid_hbm, scale,
    loss_out, gh_out, ghead_out,
    th, dh, dmap, dvalid, thead, dhead, stage, stage_big, t0, d0, a_t, a_d, map_own, map_in, sel, used,
    tp0, tp1, tp2, tr0, tr1, tr2, tfull, dp, dr, ld, s_out, s_in, st_own, st_in, f1, f2, c1, c2,
    ga_t, ga_d, keep_t, keep_d, js_t, js_d, jr_t, jr_d, q_t, q_d, qr_t, qr_d,
    w_out, w_in, ghead,
    sem_head, sem_l1s, sem_l1r, sem_rs, sem_rr, sem_sibs, sem_sibr, sem_ms, sem_mr,
    sem_ts, sem_tr, sem_ds, sem_dr, sem_ss, sem_sr, sem_fs, sem_fr, sem_cs, sem_cr,
    sem_gs, sem_gr, sem_js, sem_jr, sem_qs, sem_qr, sem_ws, sem_wr, sem_out,
):
    V, X, Z, Y, R0, G, nk, W, H, W2 = s.V, s.X, s.Z, s.Y, s.R0, s.G, s.nk, s.W, s.H, s.W2
    v = lax.axis_index("vocab")
    x = lax.axis_index("rows")
    c = lax.rem(v, 2)
    chip = lax.div(v, 2)
    y = lax.rem(chip, Y)
    z = lax.div(chip, Y)
    sib = v + 1 - 2 * c

    def at(zz, yy, cc):
        return (zz * Y + yy) * 2 + cc

    def y_peer(k):
        return at(z, lax.rem(y + k, Y), c)

    def z_peer(k):
        return at(lax.rem(z + k, Z), y, c)

    def x_peer(k):
        return lax.rem(x + k, X)

    def rcopy(src, dst, ssem, rsem, vv, xx):
        return pltpu.make_async_remote_copy(
            src_ref=src, dst_ref=dst, send_sem=ssem, recv_sem=rsem,
            device_id=(vv, xx), device_id_type=MESH,
        )

    tp, tr = (tp0, tp1, tp2), (tr0, tr1, tr2)
    sends = []
    drains = []

    def send(src, dst, ssem, rsem, vv, xx=None):
        cp = rcopy(src, dst, ssem, rsem, vv, x if xx is None else xx)
        cp.start()
        sends.append(cp)

    def arrived(dst, rsem):
        rcopy(dst, dst, rsem, rsem, sib, x).wait_recv()

    def finish():
        for cp in sends:
            cp.wait_send()
        for drain in drains:
            drain()

    owner = v < V // 2
    owner_of = lax.div(v, 2)

    barrier = pltpu.get_barrier_semaphore()

    def hello(vv, xx):
        pl.semaphore_signal(barrier, inc=1, device_id=(vv, xx), device_id_type=MESH)

    @pl.when(v > 0)
    def _():
        hello(owner_of, x)

    @pl.when(owner)
    def _():
        hello(2 * v + 1, x)

    @pl.when(jnp.logical_and(owner, v > 0))
    def _():
        hello(2 * v, x)

    for k in far_first(Y):
        for core in (0, 1):
            hello(at(z, lax.rem(y + k, Y), core), x)
    for k in far_first(Z):
        hello(z_peer(k), x)
    hello(sib, x)
    for k in range(1, X):
        hello(v, x_peer(k))

    small = [
        pltpu.make_async_copy(src, dst, sem_head.at[2 + i])
        for i, (src, dst) in enumerate(
            ((th_hbm, th), (dh_hbm, dh), (dmap_hbm, dmap), (dvalid_hbm, dvalid))
        )
    ]
    for cp in small:
        cp.start()
    load_t = pltpu.make_async_copy(thead_hbm, thead, sem_head.at[0])
    load_d = pltpu.make_async_copy(dhead_hbm, dhead, sem_head.at[1])
    load_t.start()
    load_d.start()

    for cp in small:
        cp.wait()

    for ref, dst, slot in ((th, t0, z), (dh, d0, y)):
        for k in range(nk):
            for a in range(W // L):
                cols = slice(k * W + a * L, k * W + (a + 1) * L)
                stage[a, pl.ds(k, R0, stride=nk), :] = ref[:, cols].astype(F32)
        for a in range(W // L):
            dst[slot, :, a * L:(a + 1) * L] = stage[a].astype(BF)
    masked_map = jnp.where(dvalid[...] > 0, dmap[...], -1)
    map_own[...] = jnp.broadcast_to(masked_map, map_own.shape)

    live_owner = owner.astype(jnp.int32)
    live_v = (v > 0).astype(jnp.int32)
    pl.semaphore_wait(
        barrier, 2 * (Y - 1) + (Z - 1) + 1 + (X - 1) + live_v + live_owner * (1 + live_v)
    )

    for k in far_first(Z):
        send(t0.at[z], t0.at[z], sem_l1s.at[0, k], sem_l1r.at[0, k], z_peer(k))
        send(d0.at[y], d0.at[y], sem_l1s.at[1, k], sem_l1r.at[1, k], y_peer(k))

    @pl.when(v > 0)
    def _():
        rcopy(map_own, map_in.at[c], sem_ms, sem_mr.at[c], owner_of, x).start()

    def drain_map():
        @pl.when(v > 0)
        def _():
            rcopy(map_own, map_in.at[c], sem_ms, sem_mr.at[c], owner_of, x).wait_send()

    drains.append(drain_map)

    @pl.when(v == 0)
    def _():
        map_in[0] = map_own[...]

    def relayout(src, dst, slot):
        for i in range(Y):
            for a in range(W // L):
                stage_big[a, i * G:(i + 1) * G, :] = src[i, :, a * L:(a + 1) * L].astype(F32)
        for k in range(nk):
            for a in range(W // L):
                cols = slice(k * W + a * L, k * W + (a + 1) * L)
                dst[slot, :, cols] = stage_big[a, pl.ds(k, G, stride=nk), :].astype(BF)

    for k in range(1, Z):
        arrived(t0.at[lax.rem(z + Z - k, Z)], sem_l1r.at[0, k])
    relayout(t0, a_t, 0)

    hop = (2, -2, 1, -1, 1, -1, 2, -2)
    held = (0, 0, 0, 0, -2, 2, -2, 2)
    if Z == 8:
        first_kinds, next_kinds = (0, 1, 2, 3), {0: (4, 6), 1: (5, 7)}
        turns, stages = (0, -2, 2, -1, 1, -3, 3, 4), (0, 5, 7, 8)
    else:
        first_kinds, next_kinds = (2,), {}
        turns, stages = (0, 1), (0, 2)

    def turn_slot(ring, turn, core):
        if ring == 1:
            return lax.rem(z + turn + Z, Z) * 2 + core
        near = [i for i, other in enumerate(turns) if (other - turn) % Y == 0]
        return near[0] * 2 + (0 if core is c else 1)

    def block_of(ring, turn, kind, core):
        buf, slot = (a_t, a_d)[ring], turn_slot(ring, turn, core)
        if kind is None or kind < 6:
            return buf.at[slot]
        return buf.at[slot, :, pl.ds(0, H)] if kind == 6 else buf.at[slot, :, pl.ds(H, H)]

    def ring_send(ring, kind):
        src = block_of(ring, held[kind], kind, c)
        dst = src if ring == 1 else block_of(ring, held[kind] - hop[kind], kind, c)
        send(src, dst, sem_rs.at[ring, kind], sem_rr.at[ring, kind],
             (y_peer, z_peer)[ring](hop[kind] % Z))

    def ring_wait(ring, kind):
        arrived(block_of(ring, held[kind] - hop[kind], kind, c), sem_rr.at[ring, kind])

    def sib_turn(kind):
        return 0 if kind is None else held[kind] - hop[kind]

    def sib_send(ring, kind):
        turn, k = sib_turn(kind), 7 if kind is None else kind
        src = block_of(ring, turn, None, c)
        dst = src if ring == 1 else block_of(ring, turn, None, 1 - c)
        send(src, dst, sem_sibs.at[ring, k], sem_sibr.at[ring, k], sib)

    def sib_wait(ring, kind):
        k = 7 if kind is None else kind
        arrived(block_of(ring, sib_turn(kind), None, 1 - c), sem_sibr.at[ring, k])

    def ring_start(ring):
        for kind in first_kinds:
            ring_send(ring, kind)
        sib_send(ring, None)

    ring_start(0)
    for k in range(1, Y):
        arrived(d0.at[lax.rem(y + Y - k, Y)], sem_l1r.at[1, k])
    relayout(d0, a_d, z * 2 + c)
    ring_start(1)

    used[...] = jnp.zeros_like(used)

    @pl.when(owner)
    def _():
        arrived(map_in.at[1], sem_mr.at[1])

        @pl.when(v > 0)
        def _():
            arrived(map_in.at[0], sem_mr.at[0])

        ids = iota((s.VT, s.VD), 0) + v * s.VT
        for i in range(2):
            hit = ids == jnp.broadcast_to(map_in[i, 0:1, :], (s.VT, s.VD))
            sel[:, i * s.VD:(i + 1) * s.VD] = jnp.where(hit, 1.0, 0.0).astype(BF)
        used[...] = matmul(jnp.ones((8, 2 * s.VD), BF), sel[...], NT)

    load_t.wait()

    zpx = Z // X
    per = zpx * R0

    def target_stage(st):
        lo, hi = stages[st] * 2, stages[st + 1] * 2
        tfull[lo * G:hi * G, :] = matmul(
            a_t[lo:hi].reshape((hi - lo) * G, s.F), thead[...], NT
        )
        for b in range(lo, hi):
            for r in range(X):
                tp[st][r, (b - lo) * per:(b - lo + 1) * per, :] = tfull[
                    b * G + r * per:b * G + (r + 1) * per, :
                ]
        for k in far_first(X):
            to = lax.rem(x - k + X, X)
            send(tp[st].at[to], tr[st].at[k], sem_ts.at[st, k], sem_tr.at[st, k], v, to)

    def gather(kinds):
        for kind in kinds:
            for ring in (0, 1):
                ring_wait(ring, kind)
                for later in next_kinds.get(kind, ()):
                    ring_send(ring, later)
                if kind != 6:
                    sib_send(ring, kind if kind < 6 else 6)
        for kind in kinds:
            for ring in (0, 1):
                if kind != 7:
                    sib_wait(ring, kind)

    def draft_rows():
        whole = matmul(a_d[...].reshape(s.ROWS, s.F), dhead[...], NT)
        for zz in range(Z):
            dp[zz] = whole[zz * 2 * G:(zz + 1) * 2 * G]
        for k in far_first(X):
            to = lax.rem(x - k + X, X)
            for i in range(zpx):
                send(dp.at[to * zpx + i], dr.at[k, i], sem_ds.at[k, i], sem_dr.at[k, i], v, to)

    for ring in (0, 1):
        sib_wait(ring, None)
    gather(first_kinds)
    target_stage(0)
    load_d.wait()
    if Z == 8:
        gather((4, 5))
        target_stage(1)
        gather((6, 7))
        target_stage(2)
    draft_rows()

    live_limit = s.VT * V - s.VT // 2
    live = iota((1, s.VT), 1) + v * s.VT < live_limit
    by_stage = []
    for st in range(len(stages) - 1):
        for k in range(1, X):
            arrived(tr[st].at[k], sem_tr.at[st, k])
        lt = tp[st][x]
        for k in range(1, X):
            lt = lt + tr[st][k]
        high = jnp.max(jnp.where(live, lt, FAR_BELOW), axis=1, keepdims=True)
        grown = jnp.where(live, jnp.exp(lt - high), 0.0)
        rounded = grown.astype(BF).astype(F32)
        by_stage.append((
            high, jnp.sum(grown, axis=1, keepdims=True), rounded,
            jnp.sum(rounded * used[0:1], axis=1, keepdims=True),
        ))
    tm, ts, te, mass_here = (
        jnp.concatenate(cols, axis=0) if len(cols) > 1 else cols[0] for cols in zip(*by_stage)
    )

    lr, lz = R0.bit_length() - 1, Z.bit_length() - 1
    lx = zpx.bit_length() - 1

    def spot(src, dst):
        j_ = src & (R0 - 1)
        z_ = (src >> lr) & (zpx - 1)
        c_ = (src >> (lr + lx)) & 1
        c_ = c_ + c - 2 * c * c_
        i_ = src >> (lr + lx + 1)
        turn = jnp.zeros_like(src)
        for i, other in enumerate(turns):
            turn = jnp.where(i_ == i, other % Y, turn)
        y_ = (turn + y) & (Y - 1)
        return (((z_ * 2 + c_) * Y + y_) << lr) + j_ == dst

    eye = iota((s.CH, 128), 0) == iota((s.CH, 128), 1)
    eye_t = spot(iota((s.CH, 128), 0), iota((s.CH, 128), 1))

    def to_row(col, mask=eye):
        return jnp.sum(jnp.where(mask, col, 0.0), axis=0, keepdims=True)

    eye_hi = iota((s.CH, 128), 0) + 64 == iota((s.CH, 128), 1)

    def to_col(row, mask=eye):
        return jnp.sum(jnp.where(mask, row, 0.0), axis=1, keepdims=True)

    te16 = te.astype(BF)
    tm_row, ts_row = to_row(tm, eye_t), to_row(ts, eye_t)
    st_own[...] = tm_row

    @pl.when(owner)
    def _():
        square = (s.CH, s.CH)
        order = jnp.where(spot(iota(square, 1), iota(square, 0)), 1.0, 0.0).astype(BF)
        rows = matmul(order, te16, NN).astype(BF)
        for i in range(2):
            s_out[i] = matmul(rows, sel[:, i * s.VD:(i + 1) * s.VD], NN).astype(BF)

    def soft_copies(action):
        @pl.when(owner)
        def _():
            action(rcopy(s_out.at[1], s_in, sem_ss.at[1], sem_sr.at[0], 2 * v + 1, x))
            action(rcopy(st_own, st_in, sem_ss.at[3], sem_sr.at[1], 2 * v + 1, x))

            @pl.when(v > 0)
            def _():
                action(rcopy(s_out.at[0], s_in, sem_ss.at[0], sem_sr.at[0], 2 * v, x))
                action(rcopy(st_own, st_in, sem_ss.at[2], sem_sr.at[1], 2 * v, x))

    def soft_send():
        soft_copies(lambda cp: cp.start())
        drains.append(lambda: soft_copies(lambda cp: cp.wait_send()))

        @pl.when(v == 0)
        def _():
            s_in[...] = s_out[0]
            st_in[...] = st_own[...]

    soft_send()

    valid = dvalid[...] > 0
    blocks = []
    for i in range(zpx):
        block = dp[x * zpx + i]
        for k in range(1, X):
            arrived(dr.at[k, i], sem_dr.at[k, i])
            block = block + dr[k, i]
        blocks.append(block)
    l_d = jnp.concatenate(blocks, axis=0) if zpx > 1 else blocks[0]
    ld[...] = l_d
    dm = jnp.max(jnp.where(valid, l_d, FAR_BELOW), axis=1, keepdims=True)
    ds = jnp.sum(jnp.where(valid, jnp.exp(l_d - dm), 0.0), axis=1, keepdims=True)

    maxes = tm_row + to_row(dm, eye_hi)
    sums = ts_row + to_row(ds, eye_hi)
    masses = to_row(mass_here, eye_t)

    def all_of_y():
        own_slot = y * 2 + c
        out = [
            (at(z, lax.rem(y + k, Y), core), 2 * k + core, 2 * k + c)
            for k in far_first(Y) for core in (0, 1)
        ] + [(sib, 0, c)]
        came = [(sib - at(z, 0, 0), 1 - c)] + [
            (lax.rem(y + Y - k, Y) * 2 + core, 2 * k + core)
            for k in far_first(Y)[::-1] for core in (0, 1)
        ]
        return own_slot, 2 * Y, out, came

    def all_of_z():
        out = [(z_peer(k), k, k) for k in far_first(Z)]
        came = [(lax.rem(z + Z - k, Z), k) for k in far_first(Z)[::-1]]
        return z, Z, out, came

    hops = (all_of_y(), all_of_z())

    def exchange(h, bufs, ssem, rsem, value):
        own_slot, _, out, _ = hops[h]
        bufs[h][own_slot] = value
        for to, i, k in out:
            ref = bufs[h].at[own_slot]
            send(ref, ref, ssem.at[h, i], rsem.at[h, k], to)

    def exchange_wait(h, bufs, rsem):
        for slot, k in hops[h][3]:
            arrived(bufs[h].at[slot], rsem.at[h, k])

    stats = (f1, f2)
    exchange(0, stats, sem_fs, sem_fr, jnp.concatenate([maxes, sums, masses], axis=1))

    for h in range(2):
        buf, n = stats[h], hops[h][1]
        exchange_wait(h, stats, sem_fr)
        maxes = buf[0, :, 0:L]
        for i in range(1, n):
            maxes = jnp.maximum(maxes, buf[i, :, 0:L])
        sums, masses = jnp.zeros_like(maxes), jnp.zeros_like(maxes)
        for i in range(n):
            share = jnp.exp(buf[i, :, 0:L] - maxes)
            sums = sums + buf[i, :, L:2 * L] * share
            masses = masses + buf[i, :, 2 * L:3 * L] * share
        if h == 0:
            exchange(1, stats, sem_fs, sem_fr, jnp.concatenate([maxes, sums, masses], axis=1))

    @pl.when(v > 0)
    def _():
        arrived(s_in, sem_sr.at[0])
        arrived(st_in, sem_sr.at[1])

    t_total = to_col(sums)
    factor = jnp.exp(to_col(st_in[...]) - to_col(maxes)) / t_total
    mass = to_col(masses) / t_total
    lse = to_col(maxes, eye_hi) + jnp.log(to_col(sums, eye_hi))
    soft = s_in[...].astype(F32) * factor
    l_d = ld[...]
    grad = scale[0, 0] * (jnp.exp(l_d - lse) * mass - soft)
    ga_t[pl.ds(x * s.SPC, s.SPC)] = (
        jnp.where(valid, grad, 0.0).astype(BF).reshape(s.SPC, G, s.VD)
    )
    for k in far_first(X):
        chunk = ga_t.at[pl.ds(x * s.SPC, s.SPC)]
        send(chunk, chunk, sem_gs.at[k], sem_gr.at[k], v, x_peer(k))

    cross = to_row(jnp.sum(soft * l_d, axis=1, keepdims=True))

    cross_bufs = (c1, c2)

    def cross_send(h, value):
        exchange(h, cross_bufs, sem_cs, sem_cr, value)

    def cross_wait(h):
        exchange_wait(h, cross_bufs, sem_cr)
        total = cross_bufs[h][0]
        for i in range(1, hops[h][1]):
            total = total + cross_bufs[h][i]
        return total

    cross_send(0, cross)
    shape = (s.ROWS, s.ROWS)
    dpos, tpos = iota(shape, 0), iota(shape, 1)
    dj = dpos & (R0 - 1)
    dz = (dpos >> lr) & (Z - 1)
    dc = (dpos >> (lr + lz)) & 1
    dy = dpos >> (lr + lz + 1)
    perm = jnp.where((((dz * 2 + dc) * Y + dy) << lr) + dj == tpos, 1.0, 0.0).astype(BF)

    for k in range(1, X):
        other = ga_t.at[pl.ds(lax.rem(x + X - k, X) * s.SPC, s.SPC)]
        arrived(other, sem_gr.at[k])
    def rows_of(buf, core):
        return jnp.concatenate([buf[i * 2 + core] for i in range(Z)], axis=0)

    js_t[...] = matmul(rows_of(ga_t, 1 - c), dhead[:, :H], NN).astype(BF).reshape(Z, G, H)
    send(js_t, jr_t, sem_js.at[0], sem_jr.at[0], sib)
    keep_t[...] = matmul(rows_of(ga_t, c), dhead[:, :H], NN).reshape(Z, G, H)
    ga_d[...] = (
        matmul(perm, ga_t[...].reshape(s.ROWS, s.VD), NN).astype(BF).reshape(2 * Y, G, s.VD)
    )
    js_d[...] = matmul(rows_of(ga_d, 1 - c), dhead[:, H:], NN).astype(BF).reshape(Y, G, H)
    send(js_d, jr_d, sem_js.at[1], sem_jr.at[1], sib)
    keep_d[...] = matmul(rows_of(ga_d, c), dhead[:, H:], NN).reshape(Y, G, H)

    parts = (
        (0, jr_t, keep_t, q_t, qr_t, z, Z, z_peer, y, Y, y_peer),
        (1, jr_d, keep_d, q_d, qr_d, y, Y, y_peer, z, Z, z_peer),
    )
    for i, jr, keep, q, qr, pos, n, peer, _, _, _ in parts:
        arrived(jr, sem_jr.at[i])
        for k in far_first(n):
            to = lax.rem(pos + k, n)
            q[k] = (keep[to] + jr[to].astype(F32)).astype(BF)
            send(q.at[k], qr.at[k], sem_qs.at[i, k], sem_qr.at[i, k], peer(k))

    ghead[...] = matmul(ga_t[...].reshape(s.ROWS, s.VD), a_d[...].reshape(s.ROWS, s.F), TN).astype(
        BF
    )
    store = pltpu.make_async_copy(ghead, ghead_out, sem_out)
    store.start()

    cross_send(1, cross_wait(0))

    for i, jr, keep, q, qr, pos, n, peer, pos2, n2, peer2 in parts:
        total = keep[pos] + jr[pos].astype(F32)
        for k in far_first(n)[::-1]:
            arrived(qr.at[k], sem_qr.at[i, k])
            total = total + qr[k].astype(F32)
        for k in range(nk):
            stage_big[0, pl.ds(k, G, stride=nk), :] = total[:, k * W2:(k + 1) * W2]
        for p in range(n2):
            w_out[i, p] = stage_big[0, p * G:(p + 1) * G, :].astype(BF)
        for k in far_first(n2):
            send(
                w_out.at[i, lax.rem(pos2 + k, n2)], w_in.at[i, k],
                sem_ws.at[i, k], sem_wr.at[i, k], peer2(k),
            )
        w_in[i, 0] = w_out[i, pos2]

    total_cross = to_col(cross_wait(1))
    loss = mass * lse - total_cross
    shape = (s.CH, s.CH)
    src, dst = iota(shape, 0), iota(shape, 1)
    sj = src & (R0 - 1)
    sy = (src >> lr) & (Y - 1)
    sc = (src >> (lr + lz)) & 1
    sz = src >> (lr + lz + 1)
    place = (((sz * Y + sy) * 2 + sc) << lr) + sj == dst
    loss_out[...] = jnp.sum(jnp.where(place, loss, 0.0), axis=0, keepdims=True)

    for i, jr, keep, q, qr, pos, n, peer, pos2, n2, peer2 in parts:
        total = w_in[i, 0].astype(F32)
        for k in range(1, n2):
            arrived(w_in.at[i, k], sem_wr.at[i, k])
            total = total + w_in[i, k].astype(F32)
        stage[0] = total
        for k in range(nk):
            gh_out[:, i * H + k * W2:i * H + (k + 1) * W2] = stage[
                0, pl.ds(k, R0, stride=nk), :
            ].astype(BF)

    finish()
    store.wait()


def on_device(vocab, rows, th, thead, dh, dhead, dmap, dvalid, scale):
    s = Sizes(vocab, rows, th.shape, thead.shape, dhead.shape)
    Z, Y, X, G, F, H, W, W2, VT, VD, CH = (
        s.Z, s.Y, s.X, s.G, s.F, s.H, s.W, s.W2, s.VT, s.VD, s.CH
    )
    vm = pltpu.VMEM
    dma = pltpu.SemaphoreType.DMA
    stage_rows = (40, 16, 8) if Z == 8 else (CH, 8, 8)
    scratch = [
        vm((s.R0, F), BF), vm((s.R0, F), BF),
        vm((1, VD), jnp.int32), vm((1, VD), jnp.int32),
        vm((VT, F), BF), vm((VD, F), BF),
        vm((W // L, G, L), F32), vm((W // L, G * Y, L), F32),
        vm((Y, G, W), BF), vm((Z, G, W), BF),
        vm((2 * Z, G, F), BF), vm((2 * Y, G, F), BF),
        vm((8, VD), jnp.int32), vm((2, 8, VD), jnp.int32),
        vm((VT, 2 * VD), BF), vm((8, VT), F32),
        *[vm((X, n, VT), F32) for n in stage_rows * 2],
        vm((s.ROWS, VT), F32),
        vm((Z, 2 * G, VD), F32), vm((X, Z // X, 2 * G, VD), F32),
        vm((CH, VD), F32),
        vm((2, CH, VD), BF), vm((CH, VD), BF),
        vm((1, 128), F32), vm((1, 128), F32),
        vm((2 * Y, 1, 3 * L), F32), vm((Z, 1, 3 * L), F32),
        vm((2 * Y, 1, L), F32), vm((Z, 1, L), F32),
        vm((2 * Z, G, VD), BF), vm((2 * Y, G, VD), BF),
        vm((Z, G, H), F32), vm((Y, G, H), F32),
        vm((Z, G, H), BF), vm((Y, G, H), BF),
        vm((Z, G, H), BF), vm((Y, G, H), BF),
        vm((Z, G, H), BF), vm((Y, G, H), BF),
        vm((Z, G, H), BF), vm((Y, G, H), BF),
        vm((2, Y, G, W2), BF), vm((2, Y, G, W2), BF),
        vm((VD, F), BF),
        dma((6,)),
        dma((2, Y)), dma((2, Y)),
        dma((2, 8)), dma((2, 8)),
        dma((2, 8)), dma((2, 8)),
        dma, dma((2,)),
        dma((3, X)), dma((3, X)), dma((X, Z // X)), dma((X, Z // X)),
        dma((4,)), dma((2,)),
        *[dma((2, 2 * Y))] * 4,
        dma((X,)), dma((X,)),
        dma((2,)), dma((2,)), dma((2, Z)), dma((2, Z)), dma((2, Z)), dma((2, Z)),
        dma,
    ]
    hbm = pl.BlockSpec(memory_space=pltpu.HBM)
    vmem = pl.BlockSpec(memory_space=pltpu.VMEM)
    smem = pl.BlockSpec(memory_space=pltpu.SMEM)
    loss, gh, ghead = pl.pallas_call(
        functools.partial(body, s),
        out_shape=(
            jax.ShapeDtypeStruct((1, CH), F32),
            jax.ShapeDtypeStruct((s.R0, F), BF),
            jax.ShapeDtypeStruct((VD, F), BF),
        ),
        in_specs=[hbm, hbm, hbm, hbm, hbm, hbm, smem],
        out_specs=(vmem, vmem, hbm),
        scratch_shapes=scratch,
        compiler_params=pltpu.CompilerParams(
            collective_id=0, has_side_effects=True, vmem_limit_bytes=63 * 1024 * 1024
        ),
    )(th, dh, thead, dhead, dmap.reshape(1, VD), dvalid.reshape(1, VD), scale.reshape(1, 1))
    return hand_out(ghead, gh, loss)


def hand_out(*arrays):
    def copy(*refs):
        n = len(arrays)
        held, sems = refs[2 * n:3 * n], refs[3 * n]
        moves = []
        for src, mid, dst in zip(refs[:n], held, refs[n:2 * n]):
            rows = src.shape[0]
            cut = rows // 4 if rows >= 128 else rows
            for i in range(0, rows, cut):
                part = pl.ds(i, cut)
                k = len(moves)
                moves.append((
                    pltpu.make_async_copy(src.at[part], mid.at[part], sems.at[0, k]),
                    pltpu.make_async_copy(mid.at[part], dst.at[part], sems.at[1, k]),
                ))
        for come, _ in moves:
            come.start()
        for come, go in moves:
            come.wait()
            go.start()
        for _, go in moves:
            go.wait()

    hbm = pl.BlockSpec(memory_space=pltpu.HBM)
    ghead, gh, loss = pl.pallas_call(
        copy,
        out_shape=tuple(jax.ShapeDtypeStruct(a.shape, a.dtype) for a in arrays),
        in_specs=[hbm] * len(arrays),
        out_specs=(hbm,) * len(arrays),
        scratch_shapes=[
            *[pltpu.VMEM(a.shape, a.dtype) for a in arrays],
            pltpu.SemaphoreType.DMA((2, 8)),
        ],
        compiler_params=pltpu.CompilerParams(vmem_limit_bytes=63 * 1024 * 1024),
    )(*arrays)
    return loss.reshape(loss.shape[1]), gh, ghead


def solution(mesh):
    both, one = P("vocab", "rows"), P("vocab")
    return jax.shard_map(
        functools.partial(on_device, mesh.shape["vocab"], mesh.shape["rows"]),
        mesh=mesh,
        in_specs=(both, both, both, both, one, one, P()),
        out_specs=(P("rows"), both, both),
        check_vma=False,
    )
```

```python
import functools
import math

import jax
import jax.numpy as jnp
from jax import lax
from jax.experimental import pallas as pl
from jax.experimental.pallas import tpu as pltpu
from jax.sharding import PartitionSpec as P

MESH = pl.DeviceIdType.MESH
FAR_BELOW = -1e30
L = 128
NT = (((1,), (1,)), ((), ()))
TN = (((0,), (0,)), ((), ()))
NN = (((1,), (0,)), ((), ()))
BF = jnp.bfloat16
F32 = jnp.float32


def matmul(a, b, dims):
    return lax.dot_general(a, b, dims, preferred_element_type=F32)


def iota(shape, dim):
    return lax.broadcasted_iota(jnp.int32, shape, dim)


def far_first(n):
    return sorted(range(1, n), key=lambda k: -min(k, n - k))


class Sizes:
    def __init__(self, vocab, rows, th, thead, dhead):
        self.V, self.X = vocab, rows
        self.Z = self.Y = math.isqrt(vocab // 2)
        self.R0, self.F = th
        self.G = self.R0 * self.Z
        self.nk = self.G // self.R0
        self.W = self.F // self.nk
        self.H = self.F // 2
        self.W2 = self.H // self.nk
        self.VT, self.VD = thead[0], dhead[0]
        self.ROWS = self.R0 * vocab
        self.CH = self.ROWS // rows
        self.SPC = self.CH // self.G


def body(
    s,
    th_hbm, dh_hbm, thead_hbm, dhead_hbm, dmap_hbm, dvalid_hbm, scale,
    loss_out, gh_out, ghead_out,
    th, dh, dmap, dvalid, thead, dhead, stage, stage_big, t0, d0, a_t, a_d, map_own, map_in, sel, used,
    tp0, tp1, tp2, tr0, tr1, tr2, tfull, dp, dr, ld, s_out, s_in, st_own, st_in, f1, f2, c1, c2,
    ga_t, ga_d, keep_t, keep_d, js_t, js_d, jr_t, jr_d, q_t, q_d, qr_t, qr_d,
    w_out, w_in, ghead,
    sem_head, sem_l1s, sem_l1r, sem_rs, sem_rr, sem_sibs, sem_sibr, sem_ms, sem_mr,
    sem_ts, sem_tr, sem_ds, sem_dr, sem_ss, sem_sr, sem_fs, sem_fr, sem_cs, sem_cr,
    sem_gs, sem_gr, sem_js, sem_jr, sem_qs, sem_qr, sem_ws, sem_wr, sem_out,
):
    V, X, Z, Y, R0, G, nk, W, H, W2 = s.V, s.X, s.Z, s.Y, s.R0, s.G, s.nk, s.W, s.H, s.W2
    v = lax.axis_index("vocab")
    x = lax.axis_index("rows")
    c = lax.rem(v, 2)
    chip = lax.div(v, 2)
    y = lax.rem(chip, Y)
    z = lax.div(chip, Y)
    sib = v + 1 - 2 * c

    def at(zz, yy, cc):
        return (zz * Y + yy) * 2 + cc

    def y_peer(k):
        return at(z, lax.rem(y + k, Y), c)

    def z_peer(k):
        return at(lax.rem(z + k, Z), y, c)

    def x_peer(k):
        return lax.rem(x + k, X)

    def rcopy(src, dst, ssem, rsem, vv, xx):
        return pltpu.make_async_remote_copy(
            src_ref=src, dst_ref=dst, send_sem=ssem, recv_sem=rsem,
            device_id=(vv, xx), device_id_type=MESH,
        )

    tp, tr = (tp0, tp1, tp2), (tr0, tr1, tr2)
    sends = []
    drains = []

    def send(src, dst, ssem, rsem, vv, xx=None):
        cp = rcopy(src, dst, ssem, rsem, vv, x if xx is None else xx)
        cp.start()
        sends.append(cp)

    def arrived(dst, rsem):
        rcopy(dst, dst, rsem, rsem, sib, x).wait_recv()

    def finish():
        for cp in sends:
            cp.wait_send()
        for drain in drains:
            drain()

    owner = v < V // 2
    owner_of = lax.div(v, 2)

    barrier = pltpu.get_barrier_semaphore()

    def hello(vv, xx):
        pl.semaphore_signal(barrier, inc=1, device_id=(vv, xx), device_id_type=MESH)

    @pl.when(v > 0)
    def _():
        hello(owner_of, x)

    @pl.when(owner)
    def _():
        hello(2 * v + 1, x)

    @pl.when(jnp.logical_and(owner, v > 0))
    def _():
        hello(2 * v, x)

    for k in far_first(Y):
        for core in (0, 1):
            hello(at(z, lax.rem(y + k, Y), core), x)
    for k in far_first(Z):
        hello(z_peer(k), x)
    hello(sib, x)
    for k in range(1, X):
        hello(v, x_peer(k))

    small = [
        pltpu.make_async_copy(src, dst, sem_head.at[2 + i])
        for i, (src, dst) in enumerate(
            ((th_hbm, th), (dh_hbm, dh), (dmap_hbm, dmap), (dvalid_hbm, dvalid))
        )
    ]
    for cp in small:
        cp.start()
    load_t = pltpu.make_async_copy(thead_hbm, thead, sem_head.at[0])
    load_d = pltpu.make_async_copy(dhead_hbm, dhead, sem_head.at[1])
    load_t.start()
    load_d.start()

    for cp in small:
        cp.wait()

    for ref, dst, slot in ((th, t0, z), (dh, d0, y)):
        for k in range(nk):
            for a in range(W // L):
                cols = slice(k * W + a * L, k * W + (a + 1) * L)
                stage[a, pl.ds(k, R0, stride=nk), :] = ref[:, cols].astype(F32)
        for a in range(W // L):
            dst[slot, :, a * L:(a + 1) * L] = stage[a].astype(BF)
    masked_map = jnp.where(dvalid[...] > 0, dmap[...], -1)
    map_own[...] = jnp.broadcast_to(masked_map, map_own.shape)

    live_owner = owner.astype(jnp.int32)
    live_v = (v > 0).astype(jnp.int32)
    pl.semaphore_wait(
        barrier, 2 * (Y - 1) + (Z - 1) + 1 + (X - 1) + live_v + live_owner * (1 + live_v)
    )

    for k in far_first(Z):
        send(t0.at[z], t0.at[z], sem_l1s.at[0, k], sem_l1r.at[0, k], z_peer(k))
        send(d0.at[y], d0.at[y], sem_l1s.at[1, k], sem_l1r.at[1, k], y_peer(k))

    @pl.when(v > 0)
    def _():
        rcopy(map_own, map_in.at[c], sem_ms, sem_mr.at[c], owner_of, x).start()

    def drain_map():
        @pl.when(v > 0)
        def _():
            rcopy(map_own, map_in.at[c], sem_ms, sem_mr.at[c], owner_of, x).wait_send()

    drains.append(drain_map)

    @pl.when(v == 0)
    def _():
        map_in[0] = map_own[...]

    def lay(src, i):
        for a in range(W // L):
            rows = pl.ds(pl.multiple_of(i * G, G), G)
            stage_big[a, rows, :] = src[i, :, a * L:(a + 1) * L].astype(F32)

    def relayout(src, dst, slot, pos, sem):
        lay(src, pos)
        for k in far_first(Y)[::-1]:
            i = lax.rem(pos + Y - k, Y)
            arrived(src.at[i], sem.at[k])
            lay(src, i)
        for k in range(nk):
            for a in range(W // L):
                cols = slice(k * W + a * L, k * W + (a + 1) * L)
                dst[slot, :, cols] = stage_big[a, pl.ds(k, G, stride=nk), :].astype(BF)

    relayout(t0, a_t, 0, z, sem_l1r.at[0])

    hop = (2, -2, 1, -1, 1, -1, 2, -2)
    held = (0, 0, 0, 0, -2, 2, -2, 2)
    if Z == 8:
        first_kinds, next_kinds = (0, 1, 2, 3), {0: (4, 6), 1: (5, 7)}
        turns, stages = (0, -2, 2, -1, 1, -3, 3, 4), (0, 5, 7, 8)
    else:
        first_kinds, next_kinds = (2,), {}
        turns, stages = (0, 1), (0, 2)

    def turn_slot(ring, turn, core):
        if ring == 1:
            return lax.rem(z + turn + Z, Z) * 2 + core
        near = [i for i, other in enumerate(turns) if (other - turn) % Y == 0]
        return near[0] * 2 + (0 if core is c else 1)

    def block_of(ring, turn, kind, core):
        buf, slot = (a_t, a_d)[ring], turn_slot(ring, turn, core)
        if kind is None or kind < 6:
            return buf.at[slot]
        return buf.at[slot, :, pl.ds(0, H)] if kind == 6 else buf.at[slot, :, pl.ds(H, H)]

    def ring_send(ring, kind):
        src = block_of(ring, held[kind], kind, c)
        dst = src if ring == 1 else block_of(ring, held[kind] - hop[kind], kind, c)
        send(src, dst, sem_rs.at[ring, kind], sem_rr.at[ring, kind],
             (y_peer, z_peer)[ring](hop[kind] % Z))

    def ring_wait(ring, kind):
        arrived(block_of(ring, held[kind] - hop[kind], kind, c), sem_rr.at[ring, kind])

    def sib_turn(kind):
        return 0 if kind is None else held[kind] - hop[kind]

    def sib_send(ring, kind):
        turn, k = sib_turn(kind), 7 if kind is None else kind
        src = block_of(ring, turn, None, c)
        dst = src if ring == 1 else block_of(ring, turn, None, 1 - c)
        send(src, dst, sem_sibs.at[ring, k], sem_sibr.at[ring, k], sib)

    def sib_wait(ring, kind):
        k = 7 if kind is None else kind
        arrived(block_of(ring, sib_turn(kind), None, 1 - c), sem_sibr.at[ring, k])

    def ring_start(ring):
        for kind in first_kinds:
            ring_send(ring, kind)
        sib_send(ring, None)

    ring_start(0)
    relayout(d0, a_d, z * 2 + c, y, sem_l1r.at[1])
    ring_start(1)

    used[...] = jnp.zeros_like(used)

    @pl.when(owner)
    def _():
        arrived(map_in.at[1], sem_mr.at[1])

        @pl.when(v > 0)
        def _():
            arrived(map_in.at[0], sem_mr.at[0])

        ids = iota((s.VT, s.VD), 0) + v * s.VT
        for i in range(2):
            hit = ids == jnp.broadcast_to(map_in[i, 0:1, :], (s.VT, s.VD))
            sel[:, i * s.VD:(i + 1) * s.VD] = jnp.where(hit, 1.0, 0.0).astype(BF)
        used[...] = matmul(jnp.ones((8, 2 * s.VD), BF), sel[...], NT)

    load_t.wait()

    zpx = Z // X
    per = zpx * R0

    def target_stage(st):
        lo, hi = stages[st] * 2, stages[st + 1] * 2
        tfull[lo * G:hi * G, :] = matmul(
            a_t[lo:hi].reshape((hi - lo) * G, s.F), thead[...], NT
        )
        for b in range(lo, hi):
            for r in range(X):
                tp[st][r, (b - lo) * per:(b - lo + 1) * per, :] = tfull[
                    b * G + r * per:b * G + (r + 1) * per, :
                ]
        for k in range(1, X):
            to = lax.rem(x - k + X, X)
            send(tp[st].at[to], tr[st].at[k], sem_ts.at[st, k], sem_tr.at[st, k], v, to)

    def gather(kinds):
        for kind in kinds:
            for ring in (0, 1):
                ring_wait(ring, kind)
                for later in next_kinds.get(kind, ()):
                    ring_send(ring, later)
                if kind != 6:
                    sib_send(ring, kind if kind < 6 else 6)
        for kind in kinds:
            for ring in (0, 1):
                if kind != 7:
                    sib_wait(ring, kind)

    def draft_rows():
        whole = matmul(a_d[...].reshape(s.ROWS, s.F), dhead[...], NT)
        for zz in range(Z):
            dp[zz] = whole[zz * 2 * G:(zz + 1) * 2 * G]
        for k in range(1, X):
            to = lax.rem(x - k + X, X)
            for i in range(zpx):
                send(dp.at[to * zpx + i], dr.at[k, i], sem_ds.at[k, i], sem_dr.at[k, i], v, to)

    for ring in (0, 1):
        sib_wait(ring, None)
    gather(first_kinds)
    target_stage(0)
    load_d.wait()
    if Z == 8:
        gather((4, 5))
        target_stage(1)
        gather((6, 7))
        target_stage(2)
    draft_rows()

    live_limit = s.VT * V - s.VT // 2
    live = iota((1, s.VT), 1) + v * s.VT < live_limit
    by_stage = []
    for st in range(len(stages) - 1):
        for k in range(1, X):
            arrived(tr[st].at[k], sem_tr.at[st, k])
        lt = tp[st][x]
        for k in range(1, X):
            lt = lt + tr[st][k]
        high = jnp.max(jnp.where(live, lt, FAR_BELOW), axis=1, keepdims=True)
        grown = jnp.where(live, jnp.exp(lt - high), 0.0)
        rounded = grown.astype(BF).astype(F32)
        by_stage.append((
            high, jnp.sum(grown, axis=1, keepdims=True), rounded,
            jnp.sum(rounded * used[0:1], axis=1, keepdims=True),
        ))
    tm, ts, te, mass_here = (
        jnp.concatenate(cols, axis=0) if len(cols) > 1 else cols[0] for cols in zip(*by_stage)
    )

    lr, lz = R0.bit_length() - 1, Z.bit_length() - 1
    lx = zpx.bit_length() - 1

    def spot(src, dst):
        j_ = src & (R0 - 1)
        z_ = (src >> lr) & (zpx - 1)
        c_ = (src >> (lr + lx)) & 1
        c_ = c_ + c - 2 * c * c_
        i_ = src >> (lr + lx + 1)
        turn = jnp.zeros_like(src)
        for i, other in enumerate(turns):
            turn = jnp.where(i_ == i, other % Y, turn)
        y_ = (turn + y) & (Y - 1)
        return (((z_ * 2 + c_) * Y + y_) << lr) + j_ == dst

    eye = iota((s.CH, 128), 0) == iota((s.CH, 128), 1)
    eye_t = spot(iota((s.CH, 128), 0), iota((s.CH, 128), 1))

    def to_row(col, mask=eye):
        return jnp.sum(jnp.where(mask, col, 0.0), axis=0, keepdims=True)

    eye_hi = iota((s.CH, 128), 0) + 64 == iota((s.CH, 128), 1)

    def to_col(row, mask=eye):
        return jnp.sum(jnp.where(mask, row, 0.0), axis=1, keepdims=True)

    te16 = te.astype(BF)
    tm_row, ts_row = to_row(tm, eye_t), to_row(ts, eye_t)
    st_own[...] = tm_row

    @pl.when(owner)
    def _():
        square = (s.CH, s.CH)
        order = jnp.where(spot(iota(square, 1), iota(square, 0)), 1.0, 0.0).astype(BF)
        rows = matmul(order, te16, NN).astype(BF)
        for i in range(2):
            s_out[i] = matmul(rows, sel[:, i * s.VD:(i + 1) * s.VD], NN).astype(BF)

    def soft_copies(action):
        @pl.when(owner)
        def _():
            action(rcopy(s_out.at[1], s_in, sem_ss.at[1], sem_sr.at[0], 2 * v + 1, x))
            action(rcopy(st_own, st_in, sem_ss.at[3], sem_sr.at[1], 2 * v + 1, x))

            @pl.when(v > 0)
            def _():
                action(rcopy(s_out.at[0], s_in, sem_ss.at[0], sem_sr.at[0], 2 * v, x))
                action(rcopy(st_own, st_in, sem_ss.at[2], sem_sr.at[1], 2 * v, x))

    def soft_send():
        soft_copies(lambda cp: cp.start())
        drains.append(lambda: soft_copies(lambda cp: cp.wait_send()))

        @pl.when(v == 0)
        def _():
            s_in[...] = s_out[0]
            st_in[...] = st_own[...]

    soft_send()

    valid = dvalid[...] > 0
    blocks = []
    for i in range(zpx):
        block = dp[x * zpx + i]
        for k in range(1, X):
            arrived(dr.at[k, i], sem_dr.at[k, i])
            block = block + dr[k, i]
        blocks.append(block)
    l_d = jnp.concatenate(blocks, axis=0) if zpx > 1 else blocks[0]
    ld[...] = l_d
    dm = jnp.max(jnp.where(valid, l_d, FAR_BELOW), axis=1, keepdims=True)
    ds = jnp.sum(jnp.where(valid, jnp.exp(l_d - dm), 0.0), axis=1, keepdims=True)

    maxes = tm_row + to_row(dm, eye_hi)
    sums = ts_row + to_row(ds, eye_hi)
    masses = to_row(mass_here, eye_t)

    def all_of_y():
        own_slot = y * 2 + c
        out = [
            (at(z, lax.rem(y + k, Y), core), 2 * k + core, 2 * k + c)
            for k in far_first(Y) for core in (0, 1)
        ] + [(sib, 0, c)]
        came = [(sib - at(z, 0, 0), 1 - c)] + [
            (lax.rem(y + Y - k, Y) * 2 + core, 2 * k + core)
            for k in far_first(Y)[::-1] for core in (0, 1)
        ]
        return own_slot, 2 * Y, out, came

    def all_of_z():
        out = [(z_peer(k), k, k) for k in far_first(Z)]
        came = [(lax.rem(z + Z - k, Z), k) for k in far_first(Z)[::-1]]
        return z, Z, out, came

    hops = (all_of_y(), all_of_z())

    def exchange(h, bufs, ssem, rsem, value):
        own_slot, _, out, _ = hops[h]
        bufs[h][own_slot] = value
        for to, i, k in out:
            ref = bufs[h].at[own_slot]
            send(ref, ref, ssem.at[h, i], rsem.at[h, k], to)

    def exchange_wait(h, bufs, rsem):
        for slot, k in hops[h][3]:
            arrived(bufs[h].at[slot], rsem.at[h, k])

    stats = (f1, f2)
    exchange(0, stats, sem_fs, sem_fr, jnp.concatenate([maxes, sums, masses], axis=1))

    for h in range(2):
        buf, n = stats[h], hops[h][1]
        exchange_wait(h, stats, sem_fr)
        maxes = buf[0, :, 0:L]
        for i in range(1, n):
            maxes = jnp.maximum(maxes, buf[i, :, 0:L])
        sums, masses = jnp.zeros_like(maxes), jnp.zeros_like(maxes)
        for i in range(n):
            share = jnp.exp(buf[i, :, 0:L] - maxes)
            sums = sums + buf[i, :, L:2 * L] * share
            masses = masses + buf[i, :, 2 * L:3 * L] * share
        if h == 0:
            exchange(1, stats, sem_fs, sem_fr, jnp.concatenate([maxes, sums, masses], axis=1))

    @pl.when(v > 0)
    def _():
        arrived(s_in, sem_sr.at[0])
        arrived(st_in, sem_sr.at[1])

    t_total = to_col(sums)
    factor = jnp.exp(to_col(st_in[...]) - to_col(maxes)) / t_total
    mass = to_col(masses) / t_total
    lse = to_col(maxes, eye_hi) + jnp.log(to_col(sums, eye_hi))
    soft = s_in[...].astype(F32) * factor
    l_d = ld[...]
    grad = scale[0, 0] * (jnp.exp(l_d - lse) * mass - soft)
    ga_t[pl.ds(x * s.SPC, s.SPC)] = (
        jnp.where(valid, grad, 0.0).astype(BF).reshape(s.SPC, G, s.VD)
    )
    for k in range(1, X):
        chunk = ga_t.at[pl.ds(x * s.SPC, s.SPC)]
        send(chunk, chunk, sem_gs.at[k], sem_gr.at[k], v, x_peer(k))

    cross = to_row(jnp.sum(soft * l_d, axis=1, keepdims=True))

    cross_bufs = (c1, c2)

    def cross_send(h, value):
        exchange(h, cross_bufs, sem_cs, sem_cr, value)

    def cross_wait(h):
        exchange_wait(h, cross_bufs, sem_cr)
        total = cross_bufs[h][0]
        for i in range(1, hops[h][1]):
            total = total + cross_bufs[h][i]
        return total

    cross_send(0, cross)
    shape = (s.ROWS, s.ROWS)
    dpos, tpos = iota(shape, 0), iota(shape, 1)
    dj = dpos & (R0 - 1)
    dz = (dpos >> lr) & (Z - 1)
    dc = (dpos >> (lr + lz)) & 1
    dy = dpos >> (lr + lz + 1)
    perm = jnp.where((((dz * 2 + dc) * Y + dy) << lr) + dj == tpos, 1.0, 0.0).astype(BF)

    for k in range(1, X):
        other = ga_t.at[pl.ds(lax.rem(x + X - k, X) * s.SPC, s.SPC)]
        arrived(other, sem_gr.at[k])
    def rows_of(buf, core):
        return jnp.concatenate([buf[i * 2 + core] for i in range(Z)], axis=0)

    js_t[...] = matmul(rows_of(ga_t, 1 - c), dhead[:, :H], NN).astype(BF).reshape(Z, G, H)
    send(js_t, jr_t, sem_js.at[0], sem_jr.at[0], sib)
    ga_d[...] = (
        matmul(perm, ga_t[...].reshape(s.ROWS, s.VD), NN).astype(BF).reshape(2 * Y, G, s.VD)
    )
    js_d[...] = matmul(rows_of(ga_d, 1 - c), dhead[:, H:], NN).astype(BF).reshape(Y, G, H)
    send(js_d, jr_d, sem_js.at[1], sem_jr.at[1], sib)
    keep_t[...] = matmul(rows_of(ga_t, c), dhead[:, :H], NN).reshape(Z, G, H)
    keep_d[...] = matmul(rows_of(ga_d, c), dhead[:, H:], NN).reshape(Y, G, H)

    parts = (
        (0, jr_t, keep_t, q_t, qr_t, z, Z, z_peer, y, Y, y_peer),
        (1, jr_d, keep_d, q_d, qr_d, y, Y, y_peer, z, Z, z_peer),
    )
    for i, jr, *_ in parts:
        arrived(jr, sem_jr.at[i])
    for k in far_first(Z):
        for i, jr, keep, q, qr, pos, n, peer, _, _, _ in parts:
            to = lax.rem(pos + k, n)
            q[k] = (keep[to] + jr[to].astype(F32)).astype(BF)
            send(q.at[k], qr.at[k], sem_qs.at[i, k], sem_qr.at[i, k], peer(k))

    ghead[...] = matmul(ga_t[...].reshape(s.ROWS, s.VD), a_d[...].reshape(s.ROWS, s.F), TN).astype(
        BF
    )
    store = pltpu.make_async_copy(ghead, ghead_out, sem_out)
    store.start()

    cross_send(1, cross_wait(0))

    for i, jr, keep, q, qr, pos, n, peer, pos2, n2, peer2 in parts:
        total = keep[pos] + jr[pos].astype(F32)
        for k in far_first(n)[::-1]:
            arrived(qr.at[k], sem_qr.at[i, k])
            total = total + qr[k].astype(F32)
        for k in range(nk):
            stage_big[0, pl.ds(k, G, stride=nk), :] = total[:, k * W2:(k + 1) * W2]
        for p in range(n2):
            w_out[i, p] = stage_big[0, p * G:(p + 1) * G, :].astype(BF)
        for k in far_first(n2):
            send(
                w_out.at[i, lax.rem(pos2 + k, n2)], w_in.at[i, k],
                sem_ws.at[i, k], sem_wr.at[i, k], peer2(k),
            )
        w_in[i, 0] = w_out[i, pos2]

    total_cross = to_col(cross_wait(1))
    loss = mass * lse - total_cross
    shape = (s.CH, s.CH)
    src, dst = iota(shape, 0), iota(shape, 1)
    sj = src & (R0 - 1)
    sy = (src >> lr) & (Y - 1)
    sc = (src >> (lr + lz)) & 1
    sz = src >> (lr + lz + 1)
    place = (((sz * Y + sy) * 2 + sc) << lr) + sj == dst
    loss_out[...] = jnp.sum(jnp.where(place, loss, 0.0), axis=0, keepdims=True)

    for i, jr, keep, q, qr, pos, n, peer, pos2, n2, peer2 in parts:
        total = w_in[i, 0].astype(F32)
        for k in range(1, n2):
            arrived(w_in.at[i, k], sem_wr.at[i, k])
            total = total + w_in[i, k].astype(F32)
        stage[0] = total
        for k in range(nk):
            gh_out[:, i * H + k * W2:i * H + (k + 1) * W2] = stage[
                0, pl.ds(k, R0, stride=nk), :
            ].astype(BF)

    finish()
    store.wait()


def on_device(vocab, rows, th, thead, dh, dhead, dmap, dvalid, scale):
    s = Sizes(vocab, rows, th.shape, thead.shape, dhead.shape)
    Z, Y, X, G, F, H, W, W2, VT, VD, CH = (
        s.Z, s.Y, s.X, s.G, s.F, s.H, s.W, s.W2, s.VT, s.VD, s.CH
    )
    vm = pltpu.VMEM
    dma = pltpu.SemaphoreType.DMA
    stage_rows = (40, 16, 8) if Z == 8 else (CH, 8, 8)
    scratch = [
        vm((s.R0, F), BF), vm((s.R0, F), BF),
        vm((1, VD), jnp.int32), vm((1, VD), jnp.int32),
        vm((VT, F), BF), vm((VD, F), BF),
        vm((W // L, G, L), F32), vm((W // L, G * Y, L), F32),
        vm((Y, G, W), BF), vm((Z, G, W), BF),
        vm((2 * Z, G, F), BF), vm((2 * Y, G, F), BF),
        vm((8, VD), jnp.int32), vm((2, 8, VD), jnp.int32),
        vm((VT, 2 * VD), BF), vm((8, VT), F32),
        *[vm((X, n, VT), F32) for n in stage_rows * 2],
        vm((s.ROWS, VT), F32),
        vm((Z, 2 * G, VD), F32), vm((X, Z // X, 2 * G, VD), F32),
        vm((CH, VD), F32),
        vm((2, CH, VD), BF), vm((CH, VD), BF),
        vm((1, 128), F32), vm((1, 128), F32),
        vm((2 * Y, 1, 3 * L), F32), vm((Z, 1, 3 * L), F32),
        vm((2 * Y, 1, L), F32), vm((Z, 1, L), F32),
        vm((2 * Z, G, VD), BF), vm((2 * Y, G, VD), BF),
        vm((Z, G, H), F32), vm((Y, G, H), F32),
        vm((Z, G, H), BF), vm((Y, G, H), BF),
        vm((Z, G, H), BF), vm((Y, G, H), BF),
        vm((Z, G, H), BF), vm((Y, G, H), BF),
        vm((Z, G, H), BF), vm((Y, G, H), BF),
        vm((2, Y, G, W2), BF), vm((2, Y, G, W2), BF),
        vm((VD, F), BF),
        dma((6,)),
        dma((2, Y)), dma((2, Y)),
        dma((2, 8)), dma((2, 8)),
        dma((2, 8)), dma((2, 8)),
        dma, dma((2,)),
        dma((3, X)), dma((3, X)), dma((X, Z // X)), dma((X, Z // X)),
        dma((4,)), dma((2,)),
        *[dma((2, 2 * Y))] * 4,
        dma((X,)), dma((X,)),
        dma((2,)), dma((2,)), dma((2, Z)), dma((2, Z)), dma((2, Z)), dma((2, Z)),
        dma,
    ]
    hbm = pl.BlockSpec(memory_space=pltpu.HBM)
    vmem = pl.BlockSpec(memory_space=pltpu.VMEM)
    smem = pl.BlockSpec(memory_space=pltpu.SMEM)
    loss, gh, ghead = pl.pallas_call(
        functools.partial(body, s),
        out_shape=(
            jax.ShapeDtypeStruct((1, CH), F32),
            jax.ShapeDtypeStruct((s.R0, F), BF),
            jax.ShapeDtypeStruct((VD, F), BF),
        ),
        in_specs=[hbm, hbm, hbm, hbm, hbm, hbm, smem],
        out_specs=(vmem, vmem, hbm),
        scratch_shapes=scratch,
        compiler_params=pltpu.CompilerParams(
            collective_id=0, has_side_effects=True, vmem_limit_bytes=63 * 1024 * 1024
        ),
    )(th, dh, thead, dhead, dmap.reshape(1, VD), dvalid.reshape(1, VD), scale.reshape(1, 1))
    return hand_out(ghead, gh, loss)


def hand_out(*arrays):
    def copy(*refs):
        n = len(arrays)
        held, sems = refs[2 * n:3 * n], refs[3 * n]
        moves = []
        for src, mid, dst in zip(refs[:n], held, refs[n:2 * n]):
            rows = src.shape[0]
            cut = rows // 4 if rows >= 128 else rows
            for i in range(0, rows, cut):
                part = pl.ds(i, cut)
                k = len(moves)
                moves.append((
                    pltpu.make_async_copy(src.at[part], mid.at[part], sems.at[0, k]),
                    pltpu.make_async_copy(mid.at[part], dst.at[part], sems.at[1, k]),
                ))
        for come, _ in moves:
            come.start()
        for come, go in moves:
            come.wait()
            go.start()
        for _, go in moves:
            go.wait()

    hbm = pl.BlockSpec(memory_space=pltpu.HBM)
    ghead, gh, loss = pl.pallas_call(
        copy,
        out_shape=tuple(jax.ShapeDtypeStruct(a.shape, a.dtype) for a in arrays),
        in_specs=[hbm] * len(arrays),
        out_specs=(hbm,) * len(arrays),
        scratch_shapes=[
            *[pltpu.VMEM(a.shape, a.dtype) for a in arrays],
            pltpu.SemaphoreType.DMA((2, 8)),
        ],
        compiler_params=pltpu.CompilerParams(vmem_limit_bytes=63 * 1024 * 1024),
    )(*arrays)
    return loss.reshape(loss.shape[1]), gh, ghead


def solution(mesh):
    both, one = P("vocab", "rows"), P("vocab")
    return jax.shard_map(
        functools.partial(on_device, mesh.shape["vocab"], mesh.shape["rows"]),
        mesh=mesh,
        in_specs=(both, both, both, both, one, one, P()),
        out_specs=(P("rows"), both, both),
        check_vma=False,
    )
```
